512 devices in a mesh: pair: 16 (over z), section: 2 (over x_lo), shard: 16 (over x_hi, y, core).
Axes of the slice: x: 4 (x_hi: 2, x_lo: 2; x = x_hi * 2 + x_lo), y: 4, z: 16, core: 2. Of those that a mesh axis runs over, the one named last changes fastest.
Arguments:
- section_inputs: bfloat16 [2, 16384, 4096], P('section', ('pair', 'shard')), parts along dimension 1, may hold values from -72 to 72
- keys_values: bfloat16 [2, 16384, 512], P(None, ('pair', 'shard')), parts along dimension 1, may hold values from -6 to 6
- out_weight: bfloat16 [4096, 4096], P('shard', 'section'), may hold values from -0.09375 to 0.09375
Outputs:
- section_outputs: bfloat16 [2, 16384, 4096], P('section', ('pair', 'shard')), parts along dimension 1
- weight_grad: bfloat16 [65536, 4096], P(('pair', 'shard'), 'section'), parts along dimension 0
The draws below stay inside these ranges and needn't reach their ends.
There are 16 independent parts, one for each index of `pair`. The reference program is written for one: setup_inputs(seed, part) draws one part's arguments, and reference() takes and returns one part's arrays. A program takes and returns all parts, laid end to end along the dimension named above; an argument that names none is the same for every part. Nothing has to cross between parts.
All inputs are finite; a program needn't handle non-finite values.
Results may differ from the reference program's by a relative error of at most 0.018.
Values may be sent and summed in bfloat16 or wider, within the bound.
A program may use at most 64 MiB of HBM per device.

```python
import math
import jax
import jax.numpy as jnp
from jax import lax

HEAD_DIM = 128
HEADS = 32
KV_HEADS = 4
OUT_FEAT = 4096
TOK_DEV = 64
ATTN_WIDTH = 4096
TOKENS = 1024
N_SHARD = 16


def shared_keys(key):
    shape = (2, TOKENS, KV_HEADS * HEAD_DIM)
    normal_part = jnp.clip(jax.random.normal(key, shape, jnp.float32), -6.0, 6.0)
    return normal_part


def draw_keys_values(key, part):
    normal_part = shared_keys(key)
    chosen = normal_part
    return chosen.astype(jnp.bfloat16)


def draw_section_inputs(key, part):
    key = jax.random.fold_in(key, 5)
    first_key, second_key = jax.random.split(key, 2)
    shape = (TOKENS, ATTN_WIDTH)
    queries = jnp.clip(jax.random.normal(first_key, shape, jnp.float32), -6.0, 6.0)
    cotangent = jnp.clip(jax.random.normal(second_key, shape, jnp.float32), -6.0, 6.0)
    return jnp.stack([queries, cotangent]).astype(jnp.bfloat16)


def levels(stream_key, dims, pieces, least, high):
    loudness, own = 1.0, jax.random.fold_in(stream_key, 6)
    for axis_at, blocks in pieces:
        heights = jnp.exp(jax.random.uniform(jax.random.fold_in(own, axis_at), (blocks,), jnp.float32, least / len(pieces), high / len(pieces)))
        loudness = loudness * jnp.repeat(heights, dims[axis_at] // blocks).reshape([-1 if axis == axis_at else 1 for axis in range(len(dims))])
    return loudness


def noise(key, dims, spread, limit, pieces=(), kind=jnp.bfloat16):
    factor_of = levels(key, dims, pieces, -0.22, 0.18) if pieces else 1.0
    entries = jax.random.normal(key, dims, jnp.float32) * spread * factor_of
    return jnp.minimum(jnp.maximum(entries, -limit), limit).astype(kind)


def setup_inputs(seed: int = 0, part: int = 0) -> dict:
    keys = jax.random.split(jax.random.key(seed), 4)
    part_keys = jax.random.split(jax.random.fold_in(keys[3], part), 4)
    return {
        "section_inputs": draw_section_inputs(jax.random.fold_in(jax.random.fold_in(keys[3], part), 71), part),
        "keys_values": draw_keys_values(jax.random.fold_in(jax.random.fold_in(keys[3], part), 71), part),
        "out_weight": noise(keys[2], (ATTN_WIDTH, OUT_FEAT), ATTN_WIDTH ** -0.5, 0.09375, ((0, 16), (1, 2))),
    }


def attend(queries, key_rows, value_rows):
    length = queries.shape[0]
    group_size = HEADS // KV_HEADS
    query_heads = queries.reshape(length, KV_HEADS, group_size, HEAD_DIM)
    key_heads = key_rows.reshape(length, KV_HEADS, HEAD_DIM)
    value_heads = value_rows.reshape(length, KV_HEADS, HEAD_DIM)
    scores = jnp.einsum('qhgd,khd->hgqk', query_heads, key_heads, preferred_element_type=jnp.float32) / math.sqrt(HEAD_DIM)
    causal = jnp.arange(length)[:, None] >= jnp.arange(length)[None, :]
    scores = jnp.where(causal, scores, -1e+30)
    row_max = lax.optimization_barrier(jnp.max(scores, axis=-1, keepdims=True))
    shifted = jnp.exp(scores - row_max)
    probs_low = (shifted / lax.optimization_barrier(jnp.sum(shifted, axis=-1, keepdims=True))).astype(jnp.bfloat16)
    mixed = jnp.einsum('hgqk,khd->qhgd', probs_low, value_heads, preferred_element_type=jnp.float32)
    return mixed.reshape(length, HEADS * HEAD_DIM).astype(jnp.bfloat16)

def query_grad(queries, key_rows, value_rows, grad_context):
    _, pullback = jax.vjp(lambda query_part: attend(query_part, key_rows, value_rows), queries)
    return pullback(grad_context)[0]

def per_sequence(array):
    return array.reshape(N_SHARD, TOK_DEV, array.shape[-1])

def reference(section_inputs, keys_values, out_weight):
    queries = section_inputs[0]
    cotangent = section_inputs[1]
    key_seq = per_sequence(keys_values[0])
    value_seq = per_sequence(keys_values[1])
    context = jax.vmap(attend)(per_sequence(queries), key_seq, value_seq).reshape(TOKENS, ATTN_WIDTH)
    group_rows = ATTN_WIDTH // N_SHARD
    ctx_groups = context.reshape(TOKENS, N_SHARD, group_rows).transpose(1, 0, 2)
    weight_groups = out_weight.reshape(N_SHARD, group_rows, OUT_FEAT)

    def add_group(totals, pair_item):
        partial_value = jnp.dot(pair_item[0], pair_item[1], preferred_element_type=jnp.float32)
        rounded = lax.optimization_barrier(partial_value.astype(jnp.bfloat16))
        return (totals + rounded.astype(jnp.float32), None)
    totals, _ = lax.scan(add_group, jnp.zeros((TOKENS, OUT_FEAT), jnp.float32), (ctx_groups, weight_groups))
    output = totals.astype(jnp.bfloat16)
    grad_context = jnp.dot(cotangent, out_weight.T, preferred_element_type=jnp.float32).astype(jnp.bfloat16)
    weight_grad = jnp.dot(context.T, cotangent, preferred_element_type=jnp.float32).astype(jnp.bfloat16)
    grad_queries = jax.vmap(query_grad)(per_sequence(queries), key_seq, value_seq, per_sequence(grad_context))
    grad_queries = grad_queries.reshape(TOKENS, ATTN_WIDTH)
    return (jnp.stack([grad_queries, output]), weight_grad)
```

```python
import functools
import math

import jax
import jax.numpy as jnp
from jax import lax
from jax.experimental import pallas as pl
from jax.experimental.pallas import tpu as pltpu
from jax.sharding import PartitionSpec as P

HEAD_DIM = 128
GROUP = 8
KV_HEADS = 4
TOK = 64
FEAT = 256
HALF = 2048
N_TILE = 512
SCALE = 1.0 / math.sqrt(HEAD_DIM)
BF16 = jnp.bfloat16
F32 = jnp.float32
NT = (((1,), (1,)), ((), ()))


def place_of_head(head):
    shard = head // 2
    return (shard // 2) % 4, (shard // 8) * 2 + shard % 2, (head % 2) * HEAD_DIM


def kernel(
    x_ref, kv_ref, w_ref, out_ref, dw_ref,
    q_v, kv_v, w_v, probs, cs, c1, cg, ct, g, op, ra, fwd, bwd, xr, dp, dr, ds, dc, res, dw_v,
    send_sem, load_sem, g_sem, c1_sem, cg_sem, ra_sem, f_sem, b_sem, xr_sem, dr_sem, dc_sem,
):
    s = lax.axis_index("section")
    shard = lax.axis_index("shard")
    c = lax.rem(shard, 2)
    y = lax.rem(shard // 2, 4)
    xh = shard // 8
    oc, ox, osec = 1 - c, 1 - xh, 1 - s
    yp, y2, ym = lax.rem(y + 1, 4), lax.rem(y + 2, 4), lax.rem(y + 3, 4)
    first, second = s == 0, s == 1
    k_me = xh * 2 + c

    def at(xh_, y_, c_, s_):
        return {"section": s_, "shard": (xh_ * 4 + y_) * 2 + c_}

    sibling = at(xh, y, oc, s)
    up, across, down = at(xh, yp, c, s), at(xh, y2, c, s), at(xh, ym, c, s)
    row = [(dx, d_c, d_s) for d_s in (0, 1) for dx in (0, 1) for d_c in (0, 1)]
    near = {}
    for dx, d_c, d_s in row:
        near[dx, d_c, d_s] = at(ox if dx else xh, y, oc if d_c else c, d_s)
    k_at = {(dx, d_c): (ox if dx else xh) * 2 + (oc if d_c else c) for dx in (0, 1) for d_c in (0, 1)}
    columns_of = [at(a, y, c, 1) for a in (0, 1)]
    sent = {None: [], 0: [], 1: []}
    count = [0]

    def send(when, src, dst, sem, to):
        slot = count[0]
        count[0] += 1

        def copy():
            return pltpu.make_async_remote_copy(
                src_ref=src(), dst_ref=dst(), send_sem=send_sem.at[slot], recv_sem=sem(),
                device_id=to, device_id_type=pl.DeviceIdType.MESH)

        copy().start()
        sent[when].append(copy)

    def arrive(dst, sem):
        pltpu.make_async_remote_copy(
            src_ref=dst, dst_ref=dst, send_sem=send_sem.at[0], recv_sem=sem,
            device_id=sibling, device_id_type=pl.DeviceIdType.MESH).wait_recv()

    def k_own(a):
        return a * 2 + c

    def k_other(a):
        return a * 2 + oc

    def load(src, dst, i):
        return pltpu.make_async_copy(src, dst, load_sem.at[i])

    load_w = lambda: load(w_ref, w_v, 0)
    load_q = lambda: load(x_ref.at[0], q_v, 1)
    load_kv = lambda: load(kv_ref, kv_v, 2)
    load_own = lambda: load(x_ref.at[0, :, pl.ds(HALF, HALF)], g.at[k_me, y], 3)
    load_w().start()

    @pl.when(first)
    def _():
        load_kv().start()
        load_q().start()

    @pl.when(second)
    def _():
        load_own().start()

    barrier = pltpu.get_barrier_semaphore()
    for dx, d_c, d_s in row[1:]:
        pl.semaphore_signal(barrier, inc=1, device_id=at(ox if dx else xh, y, oc if d_c else c, osec if d_s else s),
                            device_id_type=pl.DeviceIdType.MESH)
    for other in (up, across, down):
        pl.semaphore_signal(barrier, inc=1, device_id=other, device_id_type=pl.DeviceIdType.MESH)
    pl.semaphore_wait(barrier, 10)

    def chunk(k, y_):
        return lambda: g.at[k, y_]

    def chunk_sem(k, y_):
        return lambda: g_sem.at[k, y_]

    def spread(when, k, src):
        send(when, src, chunk(k, y), chunk_sem(k, y), up)
        send(when, src, chunk(k, y), chunk_sem(k, y), down)
        send(when, src, chunk(k, y), chunk_sem(k, y), sibling)

    @pl.when(second)
    def _():
        low = lambda: x_ref.at[0, :, pl.ds(0, HALF)]
        high = lambda: x_ref.at[0, :, pl.ds(HALF, HALF)]
        send(1, low, chunk(k_me, y), chunk_sem(k_me, y), near[0, 0, 0])
        send(1, low, chunk(k_me, y), chunk_sem(k_me, y), near[1, 0, 0])
        send(1, high, chunk(k_me, y), chunk_sem(k_me, y), near[1, 0, 1])
        spread(1, k_me, high)

    @pl.when(first)
    def _():
        load_kv().wait()
        load_q().wait()
        causal = (lax.rem(lax.broadcasted_iota(jnp.int32, (GROUP * TOK, TOK), 0), TOK)
                  >= lax.broadcasted_iota(jnp.int32, (GROUP * TOK, TOK), 1))
        for h in (0, 2, 1, 3):
            keys = kv_v[0, :, h * HEAD_DIM:(h + 1) * HEAD_DIM]
            values = kv_v[1, :, h * HEAD_DIM:(h + 1) * HEAD_DIM]
            heads = [h * GROUP + i for i in range(GROUP)]
            queries = jnp.concatenate([q_v[:, i * HEAD_DIM:(i + 1) * HEAD_DIM] for i in heads], axis=0)
            scores = lax.dot_general(queries, keys, NT, preferred_element_type=F32) * SCALE
            scores = jnp.where(causal, scores, -1e30)
            shifted = jnp.exp(scores - jnp.max(scores, axis=-1, keepdims=True))
            weights = shifted * (1.0 / jnp.sum(shifted, axis=-1, keepdims=True))
            probs[h] = weights
            mixed = jnp.dot(weights.astype(BF16), values, preferred_element_type=F32).astype(BF16)
            for i, head in enumerate(heads):
                y_, k_, col = place_of_head(head)
                cs[y_, k_, :, col:col + HEAD_DIM] = mixed[i * TOK:(i + 1) * TOK]
        for y_, to in ((y2, across), (yp, up), (ym, down)):
            send(0, lambda y_=y_: cs.at[y_], lambda: c1.at[:, y], lambda: c1_sem.at[y], to)
        c1[:, y] = cs[y]

    @pl.when(first)
    def _():
        arrive(g.at[k_me, y], g_sem.at[k_me, y])
        spread(0, k_me, chunk(k_me, y))

    k_ox = ox * 2 + c
    arrive(g.at[k_ox, y], g_sem.at[k_ox, y])
    spread(None, k_ox, chunk(k_ox, y))

    @pl.when(first)
    def _():
        for y_ in (yp, ym, y2):
            arrive(c1.at[:, y_], c1_sem.at[y_])
        for dx, d_c, d_s in row[1:]:
            k_ = k_at[dx, d_c]
            send(0, lambda k_=k_: c1.at[k_], lambda: cg.at[k_me], lambda: cg_sem.at[k_me], near[dx, d_c, d_s])
        cg[k_me] = c1[k_me]

    def relay(k, y_, to):
        arrive(g.at[k, y_], g_sem.at[k, y_])
        if to is not None:
            send(None, chunk(k, y_), chunk(k, y_), chunk_sem(k, y_), to)
        send(None, chunk(k, y_), chunk(k, y_), chunk_sem(k, y_), sibling)

    relay(k_own(0), ym, up)
    relay(k_own(1), yp, down)

    load_w().wait()

    @pl.when(first)
    def _():
        for a, k in ((0, k_other(0)), (1, k_other(1)), (ox, k_own(ox))):
            arrive(cg.at[k], cg_sem.at[k])

    @pl.when(second)
    def _():
        for k in range(4):
            arrive(cg.at[k], cg_sem.at[k])

    def partial(k):
        block = cg[k].reshape(4 * TOK, FEAT)

        @pl.loop(0, HALF // N_TILE)
        def _(n):
            cols = pl.ds(pl.multiple_of(n * N_TILE, N_TILE), N_TILE)
            value = jnp.dot(block, w_v[:, cols], preferred_element_type=F32).astype(BF16)
            op[k, :, :, cols] = value.reshape(4, TOK, N_TILE)

    for a in (0, 1):
        partial(k_other(a))
        for y_ in (y2, yp, ym, y):
            send(None, lambda a=a, y_=y_: op.at[k_other(a), y_], lambda a=a, y_=y_: ra.at[a, y_],
                 lambda a=a, y_=y_: ra_sem.at[a, y_], sibling)
    for a in (0, 1):
        partial(k_own(a))

    def total(a, y_, extra):
        arrive(ra.at[a, y_], ra_sem.at[a, y_])
        k = k_own(a)

        @pl.loop(0, HALF // N_TILE)
        def _(n):
            cols = pl.ds(pl.multiple_of(n * N_TILE, N_TILE), N_TILE)
            value = op[k, y_, :, cols].astype(F32) + ra[a, y_, :, cols].astype(F32)
            for ref, i in extra:
                value += ref[i, :, cols].astype(F32)
            op[k, y_, :, cols] = value.astype(BF16)

    def pass_on(a, y_, buffer, sems, i, to):
        send(None, lambda: op.at[k_own(a), y_], lambda: buffer.at[i], lambda: sems.at[i], to)

    total(0, y2, [])
    pass_on(0, y2, fwd, f_sem, 0, up)
    total(1, y2, [])
    pass_on(1, y2, bwd, b_sem, 0, down)
    total(1, yp, [])
    pass_on(1, yp, fwd, f_sem, 1, up)
    total(0, ym, [])
    pass_on(0, ym, bwd, b_sem, 1, down)

    relay(k_own(1), ym, None)
    relay(k_own(0), yp, None)
    relay(k_own(0), y2, None)
    relay(k_own(1), y2, None)

    arrive(fwd.at[0], f_sem.at[0])
    total(0, yp, [(fwd, 0)])
    pass_on(0, yp, fwd, f_sem, 2, up)
    arrive(bwd.at[0], b_sem.at[0])
    total(1, ym, [(bwd, 0)])
    pass_on(1, ym, bwd, b_sem, 2, down)

    @pl.when(second)
    def _():
        load_own().wait()

    for k in (k_other(0), k_other(1)):
        for y_ in range(4):
            arrive(g.at[k, y_], g_sem.at[k, y_])

    def grad(k):
        block = g[k].reshape(4 * TOK, HALF)
        value = lax.dot_general(block, w_v[...], NT, preferred_element_type=F32)
        dp[k] = value.astype(BF16).reshape(4, TOK, FEAT)

    for dx, d_c in ((1, 1), (0, 1), (1, 0), (0, 0)):
        k_ = k_at[dx, d_c]
        grad(k_)
        src = lambda k_=k_: dp.at[k_]
        dst = lambda: dr.at[s, k_me]
        sem = lambda: dr_sem.at[s, k_me]
        if dx == 0 and d_c == 0:
            @pl.when(second)
            def _():
                send(1, src, dst, sem, near[0, 0, 0])

            @pl.when(first)
            def _():
                dr[0, k_me] = dp[k_me]
        else:
            send(None, src, dst, sem, near[dx, d_c, 0])

    ct[...] = cg[...].reshape(16 * TOK, FEAT).T

    @pl.loop(0, HALF // FEAT)
    def _(n):
        cols = pl.ds(pl.multiple_of(n * FEAT, FEAT), FEAT)
        block = g[:, :, :, cols].reshape(16 * TOK, FEAT)
        dw_v[:, cols] = jnp.dot(ct[...], block, preferred_element_type=F32).astype(BF16)

    store_dw = lambda: load(dw_v, dw_ref, 4)
    store_dw().start()

    @pl.when(first)
    def _():
        for s_ in (0, 1):
            for dx, d_c in ((1, 1), (0, 1), (1, 0), (0, 0)):
                if s_ or dx or d_c:
                    k_ = k_at[dx, d_c]
                    arrive(dr.at[s_, k_], dr_sem.at[s_, k_])
        for k in range(4):
            ds[:, k] = (dr[0, k].astype(F32) + dr[1, k].astype(F32)).astype(BF16)
        for y_, to in ((y2, across), (yp, up), (ym, down)):
            send(0, lambda y_=y_: ds.at[y_], lambda: dc.at[y], lambda: dc_sem.at[y], to)
        dc[y] = ds[y]

    for i in (1, 2):
        arrive(fwd.at[i], f_sem.at[i])
        arrive(bwd.at[i], b_sem.at[i])
    total(0, y, [(fwd, 2), (bwd, 1)])
    total(1, y, [(fwd, 1), (bwd, 2)])

    @pl.when(first)
    def _():
        for a in (0, 1):
            send(0, lambda a=a: op.at[k_own(a), y], lambda: xr.at[xh], lambda: xr_sem.at[xh], columns_of[a])

    @pl.when(second)
    def _():
        send(1, lambda: op.at[k_ox, y], lambda: xr.at[2], lambda: xr_sem.at[2], near[1, 0, 1])

    @pl.when(first)
    def _():
        for y_ in (yp, ym, y2):
            arrive(dc.at[y_], dc_sem.at[y_])
        for h in range(KV_HEADS):
            keys = kv_v[0, :, h * HEAD_DIM:(h + 1) * HEAD_DIM]
            values = kv_v[1, :, h * HEAD_DIM:(h + 1) * HEAD_DIM]
            heads = [h * GROUP + i for i in range(GROUP)]
            parts = []
            for head in heads:
                y_, k_, col = place_of_head(head)
                parts.append(dc[y_, k_, :, col:col + HEAD_DIM])
            grads = jnp.concatenate(parts, axis=0)
            grad_probs = lax.dot_general(grads, values, NT, preferred_element_type=F32)
            weights = probs[h]
            mean = jnp.sum(weights * grad_probs, axis=-1, keepdims=True)
            grad_scores = (weights * (grad_probs - mean) * SCALE).astype(BF16)
            grad_queries = jnp.dot(grad_scores, keys, preferred_element_type=F32).astype(BF16)
            for i, head in enumerate(heads):
                res[:, head * HEAD_DIM:(head + 1) * HEAD_DIM] = grad_queries[i * TOK:(i + 1) * TOK]

    @pl.when(second)
    def _():
        for i in range(3):
            arrive(xr.at[i], xr_sem.at[i])

        @pl.loop(0, HALF // N_TILE)
        def _(n):
            cols = pl.ds(pl.multiple_of(n * N_TILE, N_TILE), N_TILE)
            high = pl.ds(pl.multiple_of(HALF + n * N_TILE, N_TILE), N_TILE)
            res[:, cols] = (xr[0, :, cols].astype(F32) + xr[1, :, cols].astype(F32)).astype(BF16)
            res[:, high] = (xr[2, :, cols].astype(F32) + op[k_me, y, :, cols].astype(F32)).astype(BF16)

    store_res = lambda: load(res, out_ref.at[0], 5)
    store_res().start()

    for copy in sent[None]:
        copy().wait_send()
    for which in (0, 1):
        @pl.when(s == which)
        def _():
            for copy in sent[which]:
                copy().wait_send()
    store_dw().wait()
    store_res().wait()


def body(section_inputs, keys_values, out_weight):
    dma = pltpu.SemaphoreType.DMA
    scratch = [
        pltpu.VMEM((TOK, 4096), BF16),
        pltpu.VMEM((2, TOK, 512), BF16),
        pltpu.VMEM((FEAT, HALF), BF16),
        pltpu.VMEM((KV_HEADS, GROUP * TOK, TOK), F32),
        pltpu.VMEM((4, 4, TOK, FEAT), BF16),
        pltpu.VMEM((4, 4, TOK, FEAT), BF16),
        pltpu.VMEM((4, 4, TOK, FEAT), BF16),
        pltpu.VMEM((FEAT, 16 * TOK), BF16),
        pltpu.VMEM((4, 4, TOK, HALF), BF16),
        pltpu.VMEM((4, 4, TOK, HALF), BF16),
        pltpu.VMEM((2, 4, TOK, HALF), BF16),
        pltpu.VMEM((3, TOK, HALF), BF16),
        pltpu.VMEM((3, TOK, HALF), BF16),
        pltpu.VMEM((3, TOK, HALF), BF16),
        pltpu.VMEM((4, 4, TOK, FEAT), BF16),
        pltpu.VMEM((2, 4, 4, TOK, FEAT), BF16),
        pltpu.VMEM((4, 4, TOK, FEAT), BF16),
        pltpu.VMEM((4, 4, TOK, FEAT), BF16),
        pltpu.VMEM((TOK, 4096), BF16),
        pltpu.VMEM((FEAT, HALF), BF16),
        dma((64,)), dma((6,)), dma((4, 4)), dma((4,)), dma((4,)), dma((2, 4)), dma((3,)), dma((3,)), dma((3,)),
        dma((2, 4)), dma((4,)),
    ]
    anywhere = pl.BlockSpec(memory_space=pl.ANY)
    return pl.pallas_call(
        kernel,
        out_shape=(jax.ShapeDtypeStruct(section_inputs.shape, BF16), jax.ShapeDtypeStruct(out_weight.shape, BF16)),
        in_specs=[anywhere] * 3,
        out_specs=(anywhere, anywhere),
        scratch_shapes=scratch,
        compiler_params=pltpu.CompilerParams(
            collective_id=0, has_side_effects=True, vmem_limit_bytes=48 * 1024 * 1024),
        cost_estimate=pl.CostEstimate(flops=3 * 2 * 1024 * 256 * 2048, bytes_accessed=4 << 20, transcendentals=1 << 17),
    )(section_inputs, keys_values, out_weight)


def solution(mesh):
    placed = (
        P("section", ("pair", "shard"), None),
        P(None, ("pair", "shard"), None),
        P("shard", "section"),
    )
    return jax.shard_map(
        body,
        mesh=mesh,
        in_specs=placed,
        out_specs=(P("section", ("pair", "shard"), None), P(("pair", "shard"), "section")),
        check_vma=False,
    )
```

```python
import functools
import math

import jax
import jax.numpy as jnp
from jax import lax
from jax.experimental import pallas as pl
from jax.experimental.pallas import tpu as pltpu
from jax.sharding import PartitionSpec as P

HEAD_DIM = 128
GROUP = 8
KV_HEADS = 4
TOK = 64
FEAT = 256
HALF = 2048
XC = 256
YC = HALF - XC
PART = YC // 2
PIECES = 2
ROWS = TOK // PIECES
LIMIT = 56
ORDER = ("gy", "rA", "xA", "gA", "T", "o0", "hA", "rB", "xB", "gB", "o1", "hB", "X", "a0", "lA", "lB", "a1", "dw")
EARLY = ("r1", "s1", "cr", "r2", "s2", "cg", "px", "p0", "gY", "p1")
SCALE = 1.0 / math.sqrt(HEAD_DIM)
BF16 = jnp.bfloat16
F32 = jnp.float32
NT = (((1,), (1,)), ((), ()))


def place_of_head(head):
    shard = head // 2
    return (shard // 2) % 4, (shard // 8) * 2 + shard % 2, (head % 2) * HEAD_DIM


def kernel(
    x_ref, kv_ref, w_ref, out_ref, dw_ref,
    q_v, kv_v, w_v, probs, cs, c1, cg, ct, g, gx, sa, op, ra, fwd, bwd, xr, px, rx, xx, xf, xb, dp, dr_part, dr_sib, dr_sec, ds, dc,
    send_sem, load_sem, g_sem, gx_sem, sa_sem, c1_sem, cg_sem, ra_sem, f_sem, b_sem, xr_sem, rx_sem, xx_sem, xf_sem, xb_sem, part_sem, sib_sem, sec_sem, ds_sem, dc_sem,
):
    s = lax.axis_index("section")
    shard = lax.axis_index("shard")
    c = lax.rem(shard, 2)
    y = lax.rem(shard // 2, 4)
    xh = shard // 8
    oc, ox, osec = 1 - c, 1 - xh, 1 - s
    yp, y2, ym = lax.rem(y + 1, 4), lax.rem(y + 2, 4), lax.rem(y + 3, 4)
    y_from, y_to = lax.rem(y + 3 - 2 * xh, 4), lax.rem(y + 1 + 2 * xh, 4)
    first, second = s == 0, s == 1
    own_k = [c, 2 + c]
    other_k = [oc, 2 + oc]
    k_me, k_ox, k_sib = xh * 2 + c, ox * 2 + c, xh * 2 + oc
    near_k = [xh * 2, xh * 2 + 1]
    far_k = [ox * 2, ox * 2 + 1]

    def at(xh_, y_, c_, s_):
        return {"section": s_, "shard": (xh_ * 4 + y_) * 2 + c_}

    sibling = at(xh, y, oc, s)
    up, across, down = at(xh, yp, c, s), at(xh, y2, c, s), at(xh, ym, c, s)
    toward, backward = at(xh, y_to, c, s), at(xh, y_from, c, s)
    row = {(a, b, d): at(a, y, b, d) for a in (0, 1) for b in (0, 1) for d in (0, 1)}
    here = [at(xh, y, c, 0), at(xh, y, c, 1)]
    far = [at(ox, y, c, 0), at(ox, y, c, 1)]
    row_own = [at(a, y, c, 1) for a in (0, 1)]
    near_row = [at(xh, y, b, 0) for b in (0, 1)]
    far_row = [at(ox, y, b, 0) for b in (0, 1)]
    sent = {None: [], 0: [], 1: []}
    count = [0]

    def send(when, src, dst, sem, to):
        slot = count[0]
        count[0] += 1

        def copy():
            return pltpu.make_async_remote_copy(
                src_ref=src(), dst_ref=dst(), send_sem=send_sem.at[slot], recv_sem=sem(),
                device_id=to, device_id_type=pl.DeviceIdType.MESH)

        copy().start()
        sent[when].append(copy)

    def arrive(dst, sem):
        pltpu.make_async_remote_copy(
            src_ref=dst, dst_ref=dst, send_sem=send_sem.at[0], recv_sem=sem,
            device_id=sibling, device_id_type=pl.DeviceIdType.MESH).wait_recv()

    def load(src, dst, i):
        return pltpu.make_async_copy(src, dst, load_sem.at[i])

    load_w = lambda: load(w_ref, w_v, 0)
    load_q = lambda: load(x_ref.at[0], q_v, 1)
    load_kv = lambda: load(kv_ref, kv_v, 2)
    load_own = lambda: load(x_ref.at[0, :, pl.ds(HALF, YC)], g.at[k_me, y], 3)
    load_own_x = lambda: load(x_ref.at[0, :, pl.ds(HALF + YC, XC)], gx.at[k_me, y], 6)

    @pl.when(first)
    def _():
        load_kv().start()
        load_q().start()

    @pl.when(second)
    def _():
        load_own().start()
        load_own_x().start()

    load_w().start()
    barrier = pltpu.get_barrier_semaphore()
    for dx, d_c, d_s in [(dx, d_c, d_s) for d_s in (0, 1) for dx in (0, 1) for d_c in (0, 1)][1:]:
        pl.semaphore_signal(barrier, inc=1, device_id=at(ox if dx else xh, y, oc if d_c else c, osec if d_s else s),
                            device_id_type=pl.DeviceIdType.MESH)
    for other in (up, across, down):
        pl.semaphore_signal(barrier, inc=1, device_id=other, device_id_type=pl.DeviceIdType.MESH)
    pl.semaphore_wait(barrier, 10)

    def piece(k, y_, p):
        return lambda: g.at[k, y_, pl.ds(p * ROWS, ROWS)]

    def piece_sem(k, y_, p):
        return lambda: g_sem.at[k, y_, p]

    def push(when, k, y_, p, to, src=None):
        send(when, src or piece(k, y_, p), piece(k, y_, p), piece_sem(k, y_, p), to)

    def got(k, y_, p):
        arrive(g.at[k, y_, pl.ds(p * ROWS, ROWS)], g_sem.at[k, y_, p])

    def push_x(when, k, y_, to, src=None):
        send(when, src or (lambda: gx.at[k, y_]), lambda: gx.at[k, y_], lambda: gx_sem.at[k, y_], to)

    def push_low(y_, to, src=None):
        send(1, src or (lambda: sa.at[y_]), lambda: sa.at[y_], lambda: sa_sem.at[y_], to)

    def to_first(y_, src=None):
        for to in (here[0], far[0]):
            push_x(1, k_me, y_, to, src or (lambda: sa.at[y_]))

    def low_arrived(y_, to):
        arrive(sa.at[y_], sa_sem.at[y_])
        if to is not None:
            push_low(y_, to)
        to_first(y_)

    def high_arrived(y_, to):
        arrive(gx.at[k_me, y_], gx_sem.at[k_me, y_])
        if to is not None:
            push_x(1, k_me, y_, to)
        push_x(1, k_me, y_, far[1])
        push_x(1, k_me, y_, sibling)

    def far_arrived(y_):
        arrive(gx.at[k_ox, y_], gx_sem.at[k_ox, y_])
        push_x(1, k_ox, y_, sibling)

    def both_arrived(y_):
        for k in (k_me, k_ox):
            arrive(gx.at[k, y_], gx_sem.at[k, y_])
            push_x(0, k, y_, sibling)

    @pl.when(second)
    def _():
        low = [lambda p=p: x_ref.at[0, pl.ds(p * ROWS, ROWS), pl.ds(0, YC)] for p in range(PIECES)]
        high = [lambda p=p: x_ref.at[0, pl.ds(p * ROWS, ROWS), pl.ds(HALF, YC)] for p in range(PIECES)]
        for p in range(PIECES):
            push(1, k_me, y, p, here[0], low[p])
            push(1, k_me, y, p, far[0], low[p])
            push(1, k_me, y, p, up, high[p])
            push(1, k_me, y, p, down, high[p])
        low_x = lambda: x_ref.at[0, :, pl.ds(YC, XC)]
        high_x = lambda: x_ref.at[0, :, pl.ds(HALF + YC, XC)]
        for to in (up, down):
            push_low(y, to, low_x)
            push_x(1, k_me, y, to, high_x)
        to_first(y, low_x)
        for p in range(PIECES):
            push(1, k_me, y, p, far[1], high[p])
            push(1, k_me, y, p, sibling, high[p])
        push_x(1, k_me, y, far[1], high_x)
        push_x(1, k_me, y, sibling, high_x)

    def relay(k, y_, to):
        for p in range(PIECES):
            got(k, y_, p)
            if to is not None:
                push(None, k, y_, p, to)
            push(None, k, y_, p, sibling)

    def row_step(source, y_):
        for a in (0, 1):
            for b in (0, 1):
                send(0, lambda a=a, b=b: source(a * 2 + b), lambda: cg.at[k_me, y_], lambda: cg_sem.at[k_me, y_], row[a, b, 1])
        send(0, lambda: source(k_sib), lambda: cg.at[k_me, y_], lambda: cg_sem.at[k_me, y_], sibling)

    @pl.when(first)
    def _():
        load_kv().wait()
        load_q().wait()
        causal = (lax.rem(lax.broadcasted_iota(jnp.int32, (GROUP * TOK, TOK), 0), TOK)
                  >= lax.broadcasted_iota(jnp.int32, (GROUP * TOK, TOK), 1))
        for h in (0, 2, 1, 3):
            keys = kv_v[0, :, h * HEAD_DIM:(h + 1) * HEAD_DIM]
            values = kv_v[1, :, h * HEAD_DIM:(h + 1) * HEAD_DIM]
            heads = [h * GROUP + i for i in range(GROUP)]
            queries = jnp.concatenate([q_v[:, i * HEAD_DIM:(i + 1) * HEAD_DIM] for i in heads], axis=0)
            scores = lax.dot_general(queries, keys, NT, preferred_element_type=F32) * SCALE
            scores = jnp.where(causal, scores, -1e30)
            shifted = jnp.exp(scores - jnp.max(scores, axis=-1, keepdims=True))
            weights = shifted * (1.0 / jnp.sum(shifted, axis=-1, keepdims=True))
            probs[h] = weights
            mixed = jnp.dot(weights.astype(BF16), values, preferred_element_type=F32).astype(BF16)
            for i, head in enumerate(heads):
                y_, k_, col = place_of_head(head)
                cs[y_, k_, :, col:col + HEAD_DIM] = mixed[i * TOK:(i + 1) * TOK]
        for y_, to in ((yp, up), (ym, down), (y2, across)):
            send(0, lambda y_=y_: cs.at[y_], lambda: c1.at[:, y], lambda: c1_sem.at[y], to)
        row_step(lambda k_: cs.at[y, k_], y)
        cg[k_me, y] = cs[y, k_me]
        for y_ in (yp, ym, y2):
            arrive(c1.at[:, y_], c1_sem.at[y_])
            row_step(lambda k_, y_=y_: c1.at[k_, y_], y_)
            cg[k_me, y_] = c1[k_me, y_]
        for p in range(PIECES):
            for k in (k_me, k_ox):
                got(k, y, p)
                push(0, k, y, p, up)
                push(0, k, y, p, down)
            for k in (k_me, k_ox):
                push(0, k, y, p, sibling)

    def grad(y_):
        for k in other_k:
            for p in range(PIECES):
                got(k, y_, p)
            arrive(gx.at[k, y_], gx_sem.at[k, y_])
        block = g[:, y_].reshape(4 * TOK, YC)
        block_x = gx[:, y_].reshape(4 * TOK, XC)
        value = lax.dot_general(block, w_v[:, :YC], NT, preferred_element_type=F32)
        value += lax.dot_general(block_x, w_v[:, YC:], NT, preferred_element_type=F32)
        dp[y_] = value.reshape(4, TOK, FEAT).astype(BF16)

        @pl.when(first)
        def _():
            send(0, lambda: dp.at[y_, pl.ds(ox * 2, 2)], lambda: dr_part.at[y_], lambda: part_sem.at[y_], here[1])
            send(0, lambda: dp.at[y_, k_sib], lambda: dr_sib.at[y_], lambda: sib_sem.at[y_], sibling)

        @pl.when(second)
        def _():
            for b in (0, 1):
                send(1, lambda b=b: dp.at[y_, near_k[b]], lambda: dr_sec.at[y_, c], lambda: sec_sem.at[y_, c], near_row[b])

    def grad_far(y_):
        @pl.when(second)
        def _():
            arrive(dr_part.at[y_], part_sem.at[y_])
            for b in (0, 1):
                dr_sec[y_, b] = (dp[y_, far_k[b]].astype(F32) + dr_part[y_, b].astype(F32)).astype(BF16)
                send(1, lambda b=b: dr_sec.at[y_, b], lambda: ds.at[y_, k_me], lambda: ds_sem.at[y_, c], far_row[b])

    def grad_along_y(y_, to):
        for b in (0, 1):
            arrive(dr_sec.at[y_, b], sec_sem.at[y_, b])
            arrive(ds.at[y_, far_k[b]], ds_sem.at[y_, b])
        arrive(dr_sib.at[y_], sib_sem.at[y_])
        ds[y_, k_me] = (dp[y_, k_me].astype(F32) + dr_sec[y_, c].astype(F32)).astype(BF16)
        ds[y_, k_sib] = (dr_sib[y_].astype(F32) + dr_sec[y_, oc].astype(F32)).astype(BF16)
        if to is None:
            dc[y] = ds[y_]
        else:
            send(0, lambda: ds.at[y_], lambda: dc.at[y], lambda: dc_sem.at[y], to)

    def product(k, start, size):
        block = cg[k].reshape(4 * TOK, FEAT)
        value = jnp.dot(block, w_v[:, start:start + size], preferred_element_type=F32)
        return value.reshape(4, TOK, size).astype(BF16)

    def partial(k, n):
        op[n, k] = product(k, n * PART, PART)

    def out_x_first():
        for a in (0, 1):
            px[other_k[a]] = product(other_k[a], YC, XC)
            send(None, lambda a=a: px.at[other_k[a]], lambda a=a: rx.at[a], lambda a=a: rx_sem.at[a], sibling)
        for a in (0, 1):
            px[own_k[a]] = product(own_k[a], YC, XC)

        def total_x(a):
            arrive(rx.at[a], rx_sem.at[a])
            px[own_k[a]] = (px[own_k[a]].astype(F32) + rx[a].astype(F32)).astype(BF16)

        for a in (0, 1):
            total_x(a)

        @pl.when(first)
        def _():
            for a in (0, 1):
                send(0, lambda a=a: px.at[own_k[a]], lambda: xx.at[xh], lambda: xx_sem.at[xh], row_own[a])

        @pl.when(second)
        def _():
            send(1, lambda: px.at[k_ox], lambda: xx.at[2], lambda: xx_sem.at[2], far[1])

    def total(n, a, y_, extra):
        arrive(ra.at[n, a, y_], ra_sem.at[n, a, y_])
        k = own_k[a]
        value = op[n, k, y_].astype(F32) + ra[n, a, y_].astype(F32)
        for ref, i in extra:
            value += ref[n, i].astype(F32)
        op[n, k, y_] = value.astype(BF16)

    def pass_on(n, a, y_, buffer, sems, i, to):
        send(None, lambda: op.at[n, own_k[a], y_], lambda: buffer.at[n, i], lambda: sems.at[n, i], to)

    def out_first(n):
        total(n, 0, y2, [])
        pass_on(n, 0, y2, fwd, f_sem, 0, up)
        total(n, 1, y2, [])
        pass_on(n, 1, y2, bwd, b_sem, 0, down)

    def out_direct(n):
        total(n, 1, yp, [])
        pass_on(n, 1, yp, fwd, f_sem, 1, up)
        total(n, 0, ym, [])
        pass_on(n, 0, ym, bwd, b_sem, 1, down)

    def out_relay(n):
        arrive(fwd.at[n, 0], f_sem.at[n, 0])
        total(n, 0, yp, [(fwd, 0)])
        pass_on(n, 0, yp, fwd, f_sem, 2, up)
        arrive(bwd.at[n, 0], b_sem.at[n, 0])
        total(n, 1, ym, [(bwd, 0)])
        pass_on(n, 1, ym, bwd, b_sem, 2, down)

    def out_along_x(n):
        for i in (1, 2):
            arrive(fwd.at[n, i], f_sem.at[n, i])
            arrive(bwd.at[n, i], b_sem.at[n, i])
        total(n, 0, y, [(fwd, 2), (bwd, 1)])
        total(n, 1, y, [(fwd, 1), (bwd, 2)])

        @pl.when(first)
        def _():
            for a in (0, 1):
                send(0, lambda a=a: op.at[n, own_k[a], y], lambda: xr.at[n, xh], lambda: xr_sem.at[n, xh], row_own[a])

        @pl.when(second)
        def _():
            send(1, lambda: op.at[n, k_ox, y], lambda: xr.at[n, 2], lambda: xr_sem.at[n, 2], far[1])

    load_w().wait()

    @pl.when(second)
    def _():
        load_own().wait()
        load_own_x().wait()

    def out_half(n):
        for a in (0, 1):
            partial(other_k[a], n)
            for y_ in (y2, yp, ym, y):
                send(None, lambda a=a, y_=y_: op.at[n, other_k[a], y_], lambda a=a, y_=y_: ra.at[n, a, y_],
                     lambda a=a, y_=y_: ra_sem.at[n, a, y_], sibling)
        for a in (0, 1):
            partial(own_k[a], n)
        out_first(n)
        out_direct(n)

    def early(name):
        if name == "r1":
            relay(k_me, y_from, toward)
        elif name == "s1":
            @pl.when(second)
            def _():
                low_arrived(ym, up)
                high_arrived(yp, down)
                for p in range(PIECES):
                    got(k_ox, y, p)
                    push(1, k_ox, y, p, up)
                    push(1, k_ox, y, p, down)
                    push(1, k_ox, y, p, sibling)
        elif name == "r2":
            relay(k_ox, y_to, backward)
        elif name == "s2":
            @pl.when(first)
            def _():
                both_arrived(y)

            @pl.when(second)
            def _():
                low_arrived(yp, None)
                high_arrived(ym, None)
                far_arrived(y)
        elif name == "cr":
            @pl.when(second)
            def _():
                for y_ in (y, yp, ym, y2):
                    for k in far_k:
                        arrive(cg.at[k, y_], cg_sem.at[k, y_])
                        send(1, lambda k=k, y_=y_: cg.at[k, y_], lambda k=k, y_=y_: cg.at[k, y_],
                             lambda k=k, y_=y_: cg_sem.at[k, y_], here[0])
        elif name == "gY":
            grad(y)
        elif name == "cg":
            @pl.when(first)
            def _():
                for y_ in (y, yp, ym, y2):
                    for k in (k_sib, far_k[0], far_k[1]):
                        arrive(cg.at[k, y_], cg_sem.at[k, y_])

            @pl.when(second)
            def _():
                for y_ in (y, yp, ym, y2):
                    for k in near_k:
                        arrive(cg.at[k, y_], cg_sem.at[k, y_])
        elif name == "px":
            out_x_first()
        elif name in ("p0", "p1"):
            out_half(int(name[1]))

    for name in EARLY:
        early(name)

    def along_y(i, y_, extra, buffer, sems, slot, to):
        if i == 0:
            value = xx[0, y_].astype(F32) + xx[1, y_].astype(F32)
        else:
            value = xx[2, y_].astype(F32) + px[k_me, y_].astype(F32)
        for ref, at_ in extra:
            value += ref[at_].astype(F32)
        if to is None:
            return value.astype(BF16)
        xx[i, y_] = value.astype(BF16)
        send(1, lambda: xx.at[i, y_], lambda: buffer.at[slot], lambda: sems.at[slot], to)

    def steps(name):
        if name == "rA":
            relay(own_k[1], ym, None)
            relay(own_k[0], yp, None)
        elif name == "xA":
            @pl.when(first)
            def _():
                both_arrived(yp)
                both_arrived(ym)

            @pl.when(second)
            def _():
                low_arrived(y2, None)
                high_arrived(y2, None)
                far_arrived(yp)
                far_arrived(ym)
        elif name == "rB":
            relay(own_k[0], y2, None)
            relay(own_k[1], y2, None)
        elif name == "xB":
            @pl.when(first)
            def _():
                both_arrived(y2)

            @pl.when(second)
            def _():
                far_arrived(y2)
        elif name == "gy":
            grad_far(y)
        elif name == "gA":
            grad(yp)
            grad(ym)
        elif name == "gB":
            grad(y2)
        elif name == "hA":
            grad_far(yp)
            grad_far(ym)
        elif name == "hB":
            grad_far(y2)
        elif name == "lA":
            @pl.when(first)
            def _():
                grad_along_y(yp, up)
                grad_along_y(ym, down)
        elif name == "lB":
            @pl.when(first)
            def _():
                grad_along_y(y2, across)
                grad_along_y(y, None)
        elif name == "T":
            @pl.when(second)
            def _():
                for i in range(3):
                    arrive(xx.at[i], xx_sem.at[i])
                along_y(0, y2, [], xf, xf_sem, 0, up)
                along_y(2, y2, [], xb, xb_sem, 0, down)
                along_y(0, ym, [], xb, xb_sem, 1, down)
                along_y(2, yp, [], xf, xf_sem, 1, up)
        elif name == "X":
            @pl.when(second)
            def _():
                arrive(xf.at[0], xf_sem.at[0])
                along_y(0, yp, [(xf, 0)], xf, xf_sem, 2, up)
                arrive(xb.at[0], xb_sem.at[0])
                along_y(2, ym, [(xb, 0)], xb, xb_sem, 2, down)
        elif name in ("o0", "o1"):
            out_relay(int(name[1]))
        elif name in ("a0", "a1"):
            out_along_x(int(name[1]))
        elif name == "dw":
            ct[...] = cg[...].reshape(16 * TOK, FEAT).T
            weight_grad(g, YC, 0)
            weight_grad(gx, XC, YC)

    def weight_grad(source, size, start):
        @pl.loop(0, size // FEAT)
        def _(n):
            cols = pl.ds(pl.multiple_of(n * FEAT, FEAT), FEAT)
            place = pl.ds(pl.multiple_of(start + n * FEAT, FEAT), FEAT)
            block = source[:, :, :, cols].reshape(16 * TOK, FEAT)
            dw_ref[:, place] = jnp.dot(ct[...], block, preferred_element_type=F32).astype(BF16)

    for name in ORDER:
        steps(name)

    @pl.when(first)
    def _():
        for y_ in (yp, ym, y2):
            arrive(dc.at[y_], dc_sem.at[y_])
        for h in range(KV_HEADS):
            keys = kv_v[0, :, h * HEAD_DIM:(h + 1) * HEAD_DIM]
            values = kv_v[1, :, h * HEAD_DIM:(h + 1) * HEAD_DIM]
            heads = [h * GROUP + i for i in range(GROUP)]
            parts = []
            for head in heads:
                y_, k_, col = place_of_head(head)
                parts.append(dc[y_, k_, :, col:col + HEAD_DIM])
            grads = jnp.concatenate(parts, axis=0)
            grad_probs = lax.dot_general(grads, values, NT, preferred_element_type=F32)
            weights = probs[h]
            mean = jnp.sum(weights * grad_probs, axis=-1, keepdims=True)
            grad_scores = (weights * (grad_probs - mean) * SCALE).astype(BF16)
            grad_queries = jnp.dot(grad_scores, keys, preferred_element_type=F32).astype(BF16)
            for i, head in enumerate(heads):
                out_ref[0, :, head * HEAD_DIM:(head + 1) * HEAD_DIM] = grad_queries[i * TOK:(i + 1) * TOK]

    @pl.when(second)
    def _():
        for i in (1, 2):
            arrive(xf.at[i], xf_sem.at[i])
            arrive(xb.at[i], xb_sem.at[i])
        out_ref[0, :, YC:HALF] = along_y(0, y, [(xf, 2), (xb, 1)], None, None, None, None)
        out_ref[0, :, HALF + YC:] = along_y(2, y, [(xf, 1), (xb, 2)], None, None, None, None)
        for n in (0, 1):
            for i in range(3):
                arrive(xr.at[n, i], xr_sem.at[n, i])
            out_ref[0, :, n * PART:(n + 1) * PART] = (xr[n, 0].astype(F32) + xr[n, 1].astype(F32)).astype(BF16)
            out_ref[0, :, HALF + n * PART:HALF + (n + 1) * PART] = (xr[n, 2].astype(F32) + op[n, k_me, y].astype(F32)).astype(BF16)


    for copy in sent[None]:
        copy().wait_send()
    for which in (0, 1):
        @pl.when(s == which)
        def _():
            for copy in sent[which]:
                copy().wait_send()


def body(section_inputs, keys_values, out_weight):
    dma = pltpu.SemaphoreType.DMA
    scratch = [
        pltpu.VMEM((TOK, 4096), BF16),
        pltpu.VMEM((2, TOK, 512), BF16),
        pltpu.VMEM((FEAT, HALF), BF16),
        pltpu.VMEM((KV_HEADS, GROUP * TOK, TOK), F32),
        pltpu.VMEM((4, 4, TOK, FEAT), BF16),
        pltpu.VMEM((4, 4, TOK, FEAT), BF16),
        pltpu.VMEM((4, 4, TOK, FEAT), BF16),
        pltpu.VMEM((FEAT, 16 * TOK), BF16),
        pltpu.VMEM((4, 4, TOK, YC), BF16),
        pltpu.VMEM((4, 4, TOK, XC), BF16),
        pltpu.VMEM((4, TOK, XC), BF16),
        pltpu.VMEM((2, 4, 4, TOK, PART), BF16),
        pltpu.VMEM((2, 2, 4, TOK, PART), BF16),
        pltpu.VMEM((2, 3, TOK, PART), BF16),
        pltpu.VMEM((2, 3, TOK, PART), BF16),
        pltpu.VMEM((2, 3, TOK, PART), BF16),
        pltpu.VMEM((4, 4, TOK, XC), BF16),
        pltpu.VMEM((2, 4, TOK, XC), BF16),
        pltpu.VMEM((3, 4, TOK, XC), BF16),
        pltpu.VMEM((3, TOK, XC), BF16),
        pltpu.VMEM((3, TOK, XC), BF16),
        pltpu.VMEM((4, 4, TOK, FEAT), BF16),
        pltpu.VMEM((4, 2, TOK, FEAT), BF16),
        pltpu.VMEM((4, TOK, FEAT), BF16),
        pltpu.VMEM((4, 2, TOK, FEAT), BF16),
        pltpu.VMEM((4, 4, TOK, FEAT), BF16),
        pltpu.VMEM((4, 4, TOK, FEAT), BF16),
        dma((256,)), dma((7,)), dma((4, 4, PIECES)), dma((4, 4)), dma((4,)), dma((4,)), dma((4, 4)), dma((2, 2, 4)), dma((2, 3)), dma((2, 3)), dma((2, 3)),
        dma((2,)), dma((3,)), dma((3,)), dma((3,)),
        dma((4,)), dma((4,)), dma((4, 2)), dma((4, 2)), dma((4,)),
    ]
    anywhere = pl.BlockSpec(memory_space=pl.ANY)
    return pl.pallas_call(
        kernel,
        out_shape=(pltpu.VMEM(section_inputs.shape, BF16), pltpu.VMEM(out_weight.shape, BF16)),
        in_specs=[anywhere] * 3,
        out_specs=(pl.BlockSpec(memory_space=pltpu.VMEM), pl.BlockSpec(memory_space=pltpu.VMEM)),
        scratch_shapes=scratch,
        compiler_params=pltpu.CompilerParams(
            collective_id=0, has_side_effects=True, vmem_limit_bytes=LIMIT * 1024 * 1024),
        cost_estimate=pl.CostEstimate(flops=3 * 2 * 1024 * 256 * 2048, bytes_accessed=4 << 20, transcendentals=1 << 17),
    )(section_inputs, keys_values, out_weight)


def solution(mesh):
    placed = (
        P("section", ("pair", "shard"), None),
        P(None, ("pair", "shard"), None),
        P("shard", "section"),
    )
    return jax.shard_map(
        body,
        mesh=mesh,
        in_specs=placed,
        out_specs=(P("section", ("pair", "shard"), None), P(("pair", "shard"), "section")),
        check_vma=False,
    )
```

```python
import functools
import math

import jax
import jax.numpy as jnp
from jax import lax
from jax.experimental import pallas as pl
from jax.experimental.pallas import tpu as pltpu
from jax.sharding import PartitionSpec as P

HEAD_DIM = 128
GROUP = 8
KV_HEADS = 4
TOK = 64
FEAT = 256
HALF = 2048
XC = 256
YC = HALF - XC
PART = YC // 2
PIECES = 4
ROWS = TOK // PIECES
LIMIT = 56
ORDER = ("gy", "rA", "xA", "gA", "hA", "T", "o0", "rB", "xB", "gB", "o1", "X", "hB", "a0", "lA", "lB", "a1", "dw")
EARLY = ("r1", "s1", "cr", "r2", "s2", "cg", "px", "p0", "gY", "p1")
SCALE = 1.0 / math.sqrt(HEAD_DIM)
BF16 = jnp.bfloat16
F32 = jnp.float32
NT = (((1,), (1,)), ((), ()))


def place_of_head(head):
    shard = head // 2
    return (shard // 2) % 4, (shard // 8) * 2 + shard % 2, (head % 2) * HEAD_DIM


def kernel(
    x_ref, kv_ref, w_ref, out_ref, dw_ref,
    q_v, kv_v, w_v, probs, cs, c1, cg, ct, g, gx, sa, op, ra, fwd, bwd, xr, px, rx, xx, xf, xb, dp, dr_part, dr_sib, dr_sec, ds, dc,
    send_sem, load_sem, g_sem, gx_sem, sa_sem, c1_sem, cg_sem, ra_sem, f_sem, b_sem, xr_sem, rx_sem, xx_sem, xf_sem, xb_sem, part_sem, sib_sem, sec_sem, ds_sem, dc_sem,
):
    s = lax.axis_index("section")
    shard = lax.axis_index("shard")
    c = lax.rem(shard, 2)
    y = lax.rem(shard // 2, 4)
    xh = shard // 8
    oc, ox, osec = 1 - c, 1 - xh, 1 - s
    yp, y2, ym = lax.rem(y + 1, 4), lax.rem(y + 2, 4), lax.rem(y + 3, 4)
    y_from, y_to = lax.rem(y + 3 - 2 * xh, 4), lax.rem(y + 1 + 2 * xh, 4)
    first, second = s == 0, s == 1
    own_k = [c, 2 + c]
    other_k = [oc, 2 + oc]
    k_me, k_ox, k_sib = xh * 2 + c, ox * 2 + c, xh * 2 + oc
    near_k = [xh * 2, xh * 2 + 1]
    far_k = [ox * 2, ox * 2 + 1]

    def at(xh_, y_, c_, s_):
        return {"section": s_, "shard": (xh_ * 4 + y_) * 2 + c_}

    sibling = at(xh, y, oc, s)
    up, across, down = at(xh, yp, c, s), at(xh, y2, c, s), at(xh, ym, c, s)
    toward, backward = at(xh, y_to, c, s), at(xh, y_from, c, s)
    row = {(a, b, d): at(a, y, b, d) for a in (0, 1) for b in (0, 1) for d in (0, 1)}
    here = [at(xh, y, c, 0), at(xh, y, c, 1)]
    far = [at(ox, y, c, 0), at(ox, y, c, 1)]
    row_own = [at(a, y, c, 1) for a in (0, 1)]
    near_row = [at(xh, y, b, 0) for b in (0, 1)]
    far_row = [at(ox, y, b, 0) for b in (0, 1)]
    sent = {None: [], 0: [], 1: []}
    count = [0]

    def send(when, src, dst, sem, to):
        slot = count[0]
        count[0] += 1

        def copy():
            return pltpu.make_async_remote_copy(
                src_ref=src(), dst_ref=dst(), send_sem=send_sem.at[slot], recv_sem=sem(),
                device_id=to, device_id_type=pl.DeviceIdType.MESH)

        copy().start()
        sent[when].append(copy)

    def arrive(dst, sem):
        pltpu.make_async_remote_copy(
            src_ref=dst, dst_ref=dst, send_sem=send_sem.at[0], recv_sem=sem,
            device_id=sibling, device_id_type=pl.DeviceIdType.MESH).wait_recv()

    def load(src, dst, i):
        return pltpu.make_async_copy(src, dst, load_sem.at[i])

    load_w = lambda: load(w_ref, w_v, 0)
    load_q = lambda: load(x_ref.at[0], q_v, 1)
    load_kv = lambda: load(kv_ref, kv_v, 2)
    load_own = lambda: load(x_ref.at[0, :, pl.ds(HALF, YC)], g.at[k_me, y], 3)
    load_own_x = lambda: load(x_ref.at[0, :, pl.ds(HALF + YC, XC)], gx.at[k_me, y], 6)

    @pl.when(first)
    def _():
        load_kv().start()
        load_q().start()

    @pl.when(second)
    def _():
        load_own().start()
        load_own_x().start()

    load_w().start()
    barrier = pltpu.get_barrier_semaphore()
    for dx, d_c, d_s in [(dx, d_c, d_s) for d_s in (0, 1) for dx in (0, 1) for d_c in (0, 1)][1:]:
        pl.semaphore_signal(barrier, inc=1, device_id=at(ox if dx else xh, y, oc if d_c else c, osec if d_s else s),
                            device_id_type=pl.DeviceIdType.MESH)
    for other in (up, across, down):
        pl.semaphore_signal(barrier, inc=1, device_id=other, device_id_type=pl.DeviceIdType.MESH)
    pl.semaphore_wait(barrier, 10)

    def piece(k, y_, p):
        return lambda: g.at[k, y_, pl.ds(p * ROWS, ROWS)]

    def piece_sem(k, y_, p):
        return lambda: g_sem.at[k, y_, p]

    def push(when, k, y_, p, to, src=None):
        send(when, src or piece(k, y_, p), piece(k, y_, p), piece_sem(k, y_, p), to)

    def got(k, y_, p):
        arrive(g.at[k, y_, pl.ds(p * ROWS, ROWS)], g_sem.at[k, y_, p])

    def push_x(when, k, y_, to, src=None):
        send(when, src or (lambda: gx.at[k, y_]), lambda: gx.at[k, y_], lambda: gx_sem.at[k, y_], to)

    def push_low(y_, to, src=None):
        send(1, src or (lambda: sa.at[y_]), lambda: sa.at[y_], lambda: sa_sem.at[y_], to)

    def to_first(y_, src=None):
        for to in (here[0], far[0]):
            push_x(1, k_me, y_, to, src or (lambda: sa.at[y_]))

    def low_arrived(y_, to):
        arrive(sa.at[y_], sa_sem.at[y_])
        if to is not None:
            push_low(y_, to)
        to_first(y_)

    def high_arrived(y_, to):
        arrive(gx.at[k_me, y_], gx_sem.at[k_me, y_])
        if to is not None:
            push_x(1, k_me, y_, to)
        push_x(1, k_me, y_, far[1])
        push_x(1, k_me, y_, sibling)

    def far_arrived(y_):
        arrive(gx.at[k_ox, y_], gx_sem.at[k_ox, y_])
        push_x(1, k_ox, y_, sibling)

    def both_arrived(y_):
        for k in (k_me, k_ox):
            arrive(gx.at[k, y_], gx_sem.at[k, y_])
            push_x(0, k, y_, sibling)

    @pl.when(second)
    def _():
        low = [lambda p=p: x_ref.at[0, pl.ds(p * ROWS, ROWS), pl.ds(0, YC)] for p in range(PIECES)]
        high = [lambda p=p: x_ref.at[0, pl.ds(p * ROWS, ROWS), pl.ds(HALF, YC)] for p in range(PIECES)]
        for p in range(PIECES):
            push(1, k_me, y, p, here[0], low[p])
            push(1, k_me, y, p, far[0], low[p])
            push(1, k_me, y, p, up, high[p])
            push(1, k_me, y, p, down, high[p])
        low_x = lambda: x_ref.at[0, :, pl.ds(YC, XC)]
        high_x = lambda: x_ref.at[0, :, pl.ds(HALF + YC, XC)]
        for to in (up, down):
            push_low(y, to, low_x)
            push_x(1, k_me, y, to, high_x)
        to_first(y, low_x)
        for p in range(PIECES):
            push(1, k_me, y, p, far[1], high[p])
            push(1, k_me, y, p, sibling, high[p])
        push_x(1, k_me, y, far[1], high_x)
        push_x(1, k_me, y, sibling, high_x)

    def relay(k, y_, to):
        for p in range(PIECES):
            got(k, y_, p)
            if to is not None:
                push(None, k, y_, p, to)
            push(None, k, y_, p, sibling)

    def row_step(source, y_):
        for a in (0, 1):
            for b in (0, 1):
                send(0, lambda a=a, b=b: source(a * 2 + b), lambda: cg.at[k_me, y_], lambda: cg_sem.at[k_me, y_], row[a, b, 1])
        send(0, lambda: source(k_sib), lambda: cg.at[k_me, y_], lambda: cg_sem.at[k_me, y_], sibling)

    @pl.when(first)
    def _():
        load_kv().wait()
        load_q().wait()
        causal = (lax.rem(lax.broadcasted_iota(jnp.int32, (GROUP * TOK, TOK), 0), TOK)
                  >= lax.broadcasted_iota(jnp.int32, (GROUP * TOK, TOK), 1))
        for h in (0, 2, 1, 3):
            keys = kv_v[0, :, h * HEAD_DIM:(h + 1) * HEAD_DIM]
            values = kv_v[1, :, h * HEAD_DIM:(h + 1) * HEAD_DIM]
            heads = [h * GROUP + i for i in range(GROUP)]
            queries = jnp.concatenate([q_v[:, i * HEAD_DIM:(i + 1) * HEAD_DIM] for i in heads], axis=0)
            scores = lax.dot_general(queries, keys, NT, preferred_element_type=F32) * SCALE
            scores = jnp.where(causal, scores, -1e30)
            shifted = jnp.exp(scores - jnp.max(scores, axis=-1, keepdims=True))
            weights = shifted * (1.0 / jnp.sum(shifted, axis=-1, keepdims=True))
            probs[h] = weights
            mixed = jnp.dot(weights.astype(BF16), values, preferred_element_type=F32).astype(BF16)
            for i, head in enumerate(heads):
                y_, k_, col = place_of_head(head)
                cs[y_, k_, :, col:col + HEAD_DIM] = mixed[i * TOK:(i + 1) * TOK]
        for y_, to in ((yp, up), (ym, down), (y2, across)):
            send(0, lambda y_=y_: cs.at[y_], lambda: c1.at[:, y], lambda: c1_sem.at[y], to)
        row_step(lambda k_: cs.at[y, k_], y)
        cg[k_me, y] = cs[y, k_me]
        for y_ in (yp, ym, y2):
            arrive(c1.at[:, y_], c1_sem.at[y_])
            row_step(lambda k_, y_=y_: c1.at[k_, y_], y_)
            cg[k_me, y_] = c1[k_me, y_]
        for p in range(PIECES):
            for k in (k_me, k_ox):
                got(k, y, p)
                push(0, k, y, p, up)
                push(0, k, y, p, down)
            for k in (k_me, k_ox):
                push(0, k, y, p, sibling)

    def grad(y_):
        for k in other_k:
            for p in range(PIECES):
                got(k, y_, p)
            arrive(gx.at[k, y_], gx_sem.at[k, y_])
        block = g[:, y_].reshape(4 * TOK, YC)
        block_x = gx[:, y_].reshape(4 * TOK, XC)
        value = lax.dot_general(block, w_v[:, :YC], NT, preferred_element_type=F32)
        value += lax.dot_general(block_x, w_v[:, YC:], NT, preferred_element_type=F32)
        dp[y_] = value.reshape(4, TOK, FEAT).astype(BF16)

        @pl.when(first)
        def _():
            send(0, lambda: dp.at[y_, pl.ds(ox * 2, 2)], lambda: dr_part.at[y_], lambda: part_sem.at[y_], here[1])
            send(0, lambda: dp.at[y_, k_sib], lambda: dr_sib.at[y_], lambda: sib_sem.at[y_], sibling)

        @pl.when(second)
        def _():
            for b in (0, 1):
                send(1, lambda b=b: dp.at[y_, near_k[b]], lambda: dr_sec.at[y_, c], lambda: sec_sem.at[y_, c], near_row[b])

    def grad_far(y_):
        @pl.when(second)
        def _():
            arrive(dr_part.at[y_], part_sem.at[y_])
            for b in (0, 1):
                dr_sec[y_, b] = (dp[y_, far_k[b]].astype(F32) + dr_part[y_, b].astype(F32)).astype(BF16)
                send(1, lambda b=b: dr_sec.at[y_, b], lambda: ds.at[y_, k_me], lambda: ds_sem.at[y_, c], far_row[b])

    def grad_along_y(y_, to):
        for b in (0, 1):
            arrive(dr_sec.at[y_, b], sec_sem.at[y_, b])
            arrive(ds.at[y_, far_k[b]], ds_sem.at[y_, b])
        arrive(dr_sib.at[y_], sib_sem.at[y_])
        ds[y_, k_me] = (dp[y_, k_me].astype(F32) + dr_sec[y_, c].astype(F32)).astype(BF16)
        ds[y_, k_sib] = (dr_sib[y_].astype(F32) + dr_sec[y_, oc].astype(F32)).astype(BF16)
        if to is None:
            dc[y] = ds[y_]
        else:
            send(0, lambda: ds.at[y_], lambda: dc.at[y], lambda: dc_sem.at[y], to)

    def product(k, start, size):
        block = cg[k].reshape(4 * TOK, FEAT)
        value = jnp.dot(block, w_v[:, start:start + size], preferred_element_type=F32)
        return value.reshape(4, TOK, size).astype(BF16)

    def partial(k, n):
        op[n, k] = product(k, n * PART, PART)

    def out_x_first():
        for a in (0, 1):
            px[other_k[a]] = product(other_k[a], YC, XC)
            send(None, lambda a=a: px.at[other_k[a]], lambda a=a: rx.at[a], lambda a=a: rx_sem.at[a], sibling)
        for a in (0, 1):
            px[own_k[a]] = product(own_k[a], YC, XC)

        def total_x(a):
            arrive(rx.at[a], rx_sem.at[a])
            px[own_k[a]] = (px[own_k[a]].astype(F32) + rx[a].astype(F32)).astype(BF16)

        for a in (0, 1):
            total_x(a)

        @pl.when(first)
        def _():
            for a in (0, 1):
                send(0, lambda a=a: px.at[own_k[a]], lambda: xx.at[xh], lambda: xx_sem.at[xh], row_own[a])

        @pl.when(second)
        def _():
            send(1, lambda: px.at[k_ox], lambda: xx.at[2], lambda: xx_sem.at[2], far[1])

    def total(n, a, y_, extra):
        arrive(ra.at[n, a, y_], ra_sem.at[n, a, y_])
        k = own_k[a]
        value = op[n, k, y_].astype(F32) + ra[n, a, y_].astype(F32)
        for ref, i in extra:
            value += ref[n, i].astype(F32)
        op[n, k, y_] = value.astype(BF16)

    def pass_on(n, a, y_, buffer, sems, i, to):
        send(None, lambda: op.at[n, own_k[a], y_], lambda: buffer.at[n, i], lambda: sems.at[n, i], to)

    def out_first(n):
        total(n, 0, y2, [])
        pass_on(n, 0, y2, fwd, f_sem, 0, up)
        total(n, 1, y2, [])
        pass_on(n, 1, y2, bwd, b_sem, 0, down)

    def out_direct(n):
        total(n, 1, yp, [])
        pass_on(n, 1, yp, fwd, f_sem, 1, up)
        total(n, 0, ym, [])
        pass_on(n, 0, ym, bwd, b_sem, 1, down)

    def out_relay(n):
        arrive(fwd.at[n, 0], f_sem.at[n, 0])
        total(n, 0, yp, [(fwd, 0)])
        pass_on(n, 0, yp, fwd, f_sem, 2, up)
        arrive(bwd.at[n, 0], b_sem.at[n, 0])
        total(n, 1, ym, [(bwd, 0)])
        pass_on(n, 1, ym, bwd, b_sem, 2, down)

    def out_along_x(n):
        for i in (1, 2):
            arrive(fwd.at[n, i], f_sem.at[n, i])
            arrive(bwd.at[n, i], b_sem.at[n, i])
        total(n, 0, y, [(fwd, 2), (bwd, 1)])
        total(n, 1, y, [(fwd, 1), (bwd, 2)])

        @pl.when(first)
        def _():
            for a in (0, 1):
                send(0, lambda a=a: op.at[n, own_k[a], y], lambda: xr.at[n, xh], lambda: xr_sem.at[n, xh], row_own[a])

        @pl.when(second)
        def _():
            send(1, lambda: op.at[n, k_ox, y], lambda: xr.at[n, 2], lambda: xr_sem.at[n, 2], far[1])

    load_w().wait()

    @pl.when(second)
    def _():
        load_own().wait()
        load_own_x().wait()

    def out_half(n):
        for a in (0, 1):
            partial(other_k[a], n)
            for y_ in (y2, yp, ym, y):
                send(None, lambda a=a, y_=y_: op.at[n, other_k[a], y_], lambda a=a, y_=y_: ra.at[n, a, y_],
                     lambda a=a, y_=y_: ra_sem.at[n, a, y_], sibling)
        for a in (0, 1):
            partial(own_k[a], n)
        out_first(n)
        out_direct(n)

    def early(name):
        if name == "r1":
            relay(k_me, y_from, toward)
        elif name == "s1":
            @pl.when(second)
            def _():
                low_arrived(ym, up)
                high_arrived(yp, down)
                for p in range(PIECES):
                    got(k_ox, y, p)
                    push(1, k_ox, y, p, up)
                    push(1, k_ox, y, p, down)
                    push(1, k_ox, y, p, sibling)
        elif name == "r2":
            relay(k_ox, y_to, backward)
        elif name == "s2":
            @pl.when(first)
            def _():
                both_arrived(y)

            @pl.when(second)
            def _():
                low_arrived(yp, None)
                high_arrived(ym, None)
                far_arrived(y)
        elif name == "cr":
            @pl.when(second)
            def _():
                for y_ in (y, yp, ym, y2):
                    for k in far_k:
                        arrive(cg.at[k, y_], cg_sem.at[k, y_])
                        send(1, lambda k=k, y_=y_: cg.at[k, y_], lambda k=k, y_=y_: cg.at[k, y_],
                             lambda k=k, y_=y_: cg_sem.at[k, y_], here[0])
        elif name == "gY":
            grad(y)
        elif name == "cg":
            @pl.when(first)
            def _():
                for y_ in (y, yp, ym, y2):
                    for k in (k_sib, far_k[0], far_k[1]):
                        arrive(cg.at[k, y_], cg_sem.at[k, y_])

            @pl.when(second)
            def _():
                for y_ in (y, yp, ym, y2):
                    for k in near_k:
                        arrive(cg.at[k, y_], cg_sem.at[k, y_])
        elif name == "px":
            out_x_first()
        elif name in ("p0", "p1"):
            out_half(int(name[1]))

    for name in EARLY:
        early(name)

    def along_y(i, y_, extra, buffer, sems, slot, to):
        if i == 0:
            value = xx[0, y_].astype(F32) + xx[1, y_].astype(F32)
        else:
            value = xx[2, y_].astype(F32) + px[k_me, y_].astype(F32)
        for ref, at_ in extra:
            value += ref[at_].astype(F32)
        if to is None:
            return value.astype(BF16)
        xx[i, y_] = value.astype(BF16)
        send(1, lambda: xx.at[i, y_], lambda: buffer.at[slot], lambda: sems.at[slot], to)

    def steps(name):
        if name == "rA":
            relay(own_k[1], ym, None)
            relay(own_k[0], yp, None)
        elif name == "xA":
            @pl.when(first)
            def _():
                both_arrived(yp)
                both_arrived(ym)

            @pl.when(second)
            def _():
                low_arrived(y2, None)
                high_arrived(y2, None)
                far_arrived(yp)
                far_arrived(ym)
        elif name == "rB":
            relay(own_k[0], y2, None)
            relay(own_k[1], y2, None)
        elif name == "xB":
            @pl.when(first)
            def _():
                both_arrived(y2)

            @pl.when(second)
            def _():
                far_arrived(y2)
        elif name == "gy":
            grad_far(y)
        elif name == "gA":
            grad(yp)
            grad(ym)
        elif name == "gB":
            grad(y2)
        elif name == "hA":
            grad_far(yp)
            grad_far(ym)
        elif name == "hB":
            grad_far(y2)
        elif name == "lA":
            @pl.when(first)
            def _():
                grad_along_y(yp, up)
                grad_along_y(ym, down)
        elif name == "lB":
            @pl.when(first)
            def _():
                grad_along_y(y2, across)
                grad_along_y(y, None)
        elif name == "T":
            @pl.when(second)
            def _():
                for i in range(3):
                    arrive(xx.at[i], xx_sem.at[i])
                along_y(0, y2, [], xf, xf_sem, 0, up)
                along_y(2, y2, [], xb, xb_sem, 0, down)
                along_y(0, ym, [], xb, xb_sem, 1, down)
                along_y(2, yp, [], xf, xf_sem, 1, up)
        elif name == "X":
            @pl.when(second)
            def _():
                arrive(xf.at[0], xf_sem.at[0])
                along_y(0, yp, [(xf, 0)], xf, xf_sem, 2, up)
                arrive(xb.at[0], xb_sem.at[0])
                along_y(2, ym, [(xb, 0)], xb, xb_sem, 2, down)
        elif name in ("o0", "o1"):
            out_relay(int(name[1]))
        elif name in ("a0", "a1"):
            out_along_x(int(name[1]))
        elif name == "dw":
            ct[...] = cg[...].reshape(16 * TOK, FEAT).T
            weight_grad(g, YC, 0)
            weight_grad(gx, XC, YC)

    def weight_grad(source, size, start):
        @pl.loop(0, size // FEAT)
        def _(n):
            cols = pl.ds(pl.multiple_of(n * FEAT, FEAT), FEAT)
            place = pl.ds(pl.multiple_of(start + n * FEAT, FEAT), FEAT)
            block = source[:, :, :, cols].reshape(16 * TOK, FEAT)
            dw_ref[:, place] = jnp.dot(ct[...], block, preferred_element_type=F32).astype(BF16)

    for name in ORDER:
        steps(name)

    @pl.when(first)
    def _():
        for y_ in (yp, ym, y2):
            arrive(dc.at[y_], dc_sem.at[y_])
        for h in range(KV_HEADS):
            keys = kv_v[0, :, h * HEAD_DIM:(h + 1) * HEAD_DIM]
            values = kv_v[1, :, h * HEAD_DIM:(h + 1) * HEAD_DIM]
            heads = [h * GROUP + i for i in range(GROUP)]
            parts = []
            for head in heads:
                y_, k_, col = place_of_head(head)
                parts.append(dc[y_, k_, :, col:col + HEAD_DIM])
            grads = jnp.concatenate(parts, axis=0)
            grad_probs = lax.dot_general(grads, values, NT, preferred_element_type=F32)
            weights = probs[h]
            mean = jnp.sum(weights * grad_probs, axis=-1, keepdims=True)
            grad_scores = (weights * (grad_probs - mean) * SCALE).astype(BF16)
            grad_queries = jnp.dot(grad_scores, keys, preferred_element_type=F32).astype(BF16)
            for i, head in enumerate(heads):
                out_ref[0, :, head * HEAD_DIM:(head + 1) * HEAD_DIM] = grad_queries[i * TOK:(i + 1) * TOK]

    @pl.when(second)
    def _():
        for i in (1, 2):
            arrive(xf.at[i], xf_sem.at[i])
            arrive(xb.at[i], xb_sem.at[i])
        out_ref[0, :, YC:HALF] = along_y(0, y, [(xf, 2), (xb, 1)], None, None, None, None)
        out_ref[0, :, HALF + YC:] = along_y(2, y, [(xf, 1), (xb, 2)], None, None, None, None)
        for n in (0, 1):
            for i in range(3):
                arrive(xr.at[n, i], xr_sem.at[n, i])
            out_ref[0, :, n * PART:(n + 1) * PART] = (xr[n, 0].astype(F32) + xr[n, 1].astype(F32)).astype(BF16)
            out_ref[0, :, HALF + n * PART:HALF + (n + 1) * PART] = (xr[n, 2].astype(F32) + op[n, k_me, y].astype(F32)).astype(BF16)


    for copy in sent[None]:
        copy().wait_send()
    for which in (0, 1):
        @pl.when(s == which)
        def _():
            for copy in sent[which]:
                copy().wait_send()


def body(section_inputs, keys_values, out_weight):
    dma = pltpu.SemaphoreType.DMA
    scratch = [
        pltpu.VMEM((TOK, 4096), BF16),
        pltpu.VMEM((2, TOK, 512), BF16),
        pltpu.VMEM((FEAT, HALF), BF16),
        pltpu.VMEM((KV_HEADS, GROUP * TOK, TOK), F32),
        pltpu.VMEM((4, 4, TOK, FEAT), BF16),
        pltpu.VMEM((4, 4, TOK, FEAT), BF16),
        pltpu.VMEM((4, 4, TOK, FEAT), BF16),
        pltpu.VMEM((FEAT, 16 * TOK), BF16),
        pltpu.VMEM((4, 4, TOK, YC), BF16),
        pltpu.VMEM((4, 4, TOK, XC), BF16),
        pltpu.VMEM((4, TOK, XC), BF16),
        pltpu.VMEM((2, 4, 4, TOK, PART), BF16),
        pltpu.VMEM((2, 2, 4, TOK, PART), BF16),
        pltpu.VMEM((2, 3, TOK, PART), BF16),
        pltpu.VMEM((2, 3, TOK, PART), BF16),
        pltpu.VMEM((2, 3, TOK, PART), BF16),
        pltpu.VMEM((4, 4, TOK, XC), BF16),
        pltpu.VMEM((2, 4, TOK, XC), BF16),
        pltpu.VMEM((3, 4, TOK, XC), BF16),
        pltpu.VMEM((3, TOK, XC), BF16),
        pltpu.VMEM((3, TOK, XC), BF16),
        pltpu.VMEM((4, 4, TOK, FEAT), BF16),
        pltpu.VMEM((4, 2, TOK, FEAT), BF16),
        pltpu.VMEM((4, TOK, FEAT), BF16),
        pltpu.VMEM((4, 2, TOK, FEAT), BF16),
        pltpu.VMEM((4, 4, TOK, FEAT), BF16),
        pltpu.VMEM((4, 4, TOK, FEAT), BF16),
        dma((256,)), dma((7,)), dma((4, 4, PIECES)), dma((4, 4)), dma((4,)), dma((4,)), dma((4, 4)), dma((2, 2, 4)), dma((2, 3)), dma((2, 3)), dma((2, 3)),
        dma((2,)), dma((3,)), dma((3,)), dma((3,)),
        dma((4,)), dma((4,)), dma((4, 2)), dma((4, 2)), dma((4,)),
    ]
    anywhere = pl.BlockSpec(memory_space=pl.ANY)
    return pl.pallas_call(
        kernel,
        out_shape=(pltpu.VMEM(section_inputs.shape, BF16), pltpu.VMEM(out_weight.shape, BF16)),
        in_specs=[anywhere] * 3,
        out_specs=(pl.BlockSpec(memory_space=pltpu.VMEM), pl.BlockSpec(memory_space=pltpu.VMEM)),
        scratch_shapes=scratch,
        compiler_params=pltpu.CompilerParams(
            collective_id=0, has_side_effects=True, vmem_limit_bytes=LIMIT * 1024 * 1024),
        cost_estimate=pl.CostEstimate(flops=3 * 2 * 1024 * 256 * 2048, bytes_accessed=4 << 20, transcendentals=1 << 17),
    )(section_inputs, keys_values, out_weight)


def solution(mesh):
    placed = (
        P("section", ("pair", "shard"), None),
        P(None, ("pair", "shard"), None),
        P("shard", "section"),
    )
    return jax.shard_map(
        body,
        mesh=mesh,
        in_specs=placed,
        out_specs=(P("section", ("pair", "shard"), None), P(("pair", "shard"), "section")),
        check_vma=False,
    )
```

```python
import functools
import math

import jax
import jax.numpy as jnp
from jax import lax
from jax.experimental import pallas as pl
from jax.experimental.pallas import tpu as pltpu
from jax.sharding import PartitionSpec as P

HEAD_DIM = 128
GROUP = 8
KV_HEADS = 4
TOK = 64
FEAT = 256
HALF = 2048
XC = 256
CFIRST = True
YC = HALF - XC
PART = YC // 2
PIECES = 4
ROWS = TOK // PIECES
LIMIT = 56
ORDER = ("gy", "rA", "xA", "gA", "hA", "T", "o0", "rB", "xB", "gB", "o1", "X", "hB", "a0", "lA", "lB", "a1", "dw")
EARLY = ("r1", "s1", "cr", "r2", "s2", "px", "p0", "gY", "p1")
SCALE = 1.0 / math.sqrt(HEAD_DIM)
BF16 = jnp.bfloat16
F32 = jnp.float32
NT = (((1,), (1,)), ((), ()))


def place_of_head(head):
    shard = head // 2
    return (shard // 2) % 4, (shard // 8) * 2 + shard % 2, (head % 2) * HEAD_DIM


def kernel(
    x_ref, kv_ref, w_ref, out_ref, dw_ref,
    q_v, kv_v, w_v, probs, cs, c1, cg, ct, g, gx, sa, op, ra, fwd, bwd, xr, px, rx, xx, xf, xb, dp, dr_part, dr_sib, dr_sec, ds, dc,
    send_sem, load_sem, g_sem, gx_sem, sa_sem, c1_sem, cg_sem, ra_sem, f_sem, b_sem, xr_sem, rx_sem, xx_sem, xf_sem, xb_sem, part_sem, sib_sem, sec_sem, ds_sem, dc_sem,
):
    s = lax.axis_index("section")
    shard = lax.axis_index("shard")
    c = lax.rem(shard, 2)
    y = lax.rem(shard // 2, 4)
    xh = shard // 8
    oc, ox, osec = 1 - c, 1 - xh, 1 - s
    yp, y2, ym = lax.rem(y + 1, 4), lax.rem(y + 2, 4), lax.rem(y + 3, 4)
    y_from, y_to = lax.rem(y + 3 - 2 * xh, 4), lax.rem(y + 1 + 2 * xh, 4)
    first, second = s == 0, s == 1
    own_k = [c, 2 + c]
    other_k = [oc, 2 + oc]
    k_me, k_ox, k_sib = xh * 2 + c, ox * 2 + c, xh * 2 + oc
    near_k = [xh * 2, xh * 2 + 1]
    far_k = [ox * 2, ox * 2 + 1]

    def at(xh_, y_, c_, s_):
        return {"section": s_, "shard": (xh_ * 4 + y_) * 2 + c_}

    sibling = at(xh, y, oc, s)
    up, across, down = at(xh, yp, c, s), at(xh, y2, c, s), at(xh, ym, c, s)
    toward, backward = at(xh, y_to, c, s), at(xh, y_from, c, s)
    row = {(a, b, d): at(a, y, b, d) for a in (0, 1) for b in (0, 1) for d in (0, 1)}
    here = [at(xh, y, c, 0), at(xh, y, c, 1)]
    far = [at(ox, y, c, 0), at(ox, y, c, 1)]
    row_own = [at(a, y, c, 1) for a in (0, 1)]
    near_row = [at(xh, y, b, 0) for b in (0, 1)]
    far_row = [at(ox, y, b, 0) for b in (0, 1)]
    sent = {None: [], 0: [], 1: []}
    count = [0]

    def send(when, src, dst, sem, to):
        slot = count[0]
        count[0] += 1

        def copy():
            return pltpu.make_async_remote_copy(
                src_ref=src(), dst_ref=dst(), send_sem=send_sem.at[slot], recv_sem=sem(),
                device_id=to, device_id_type=pl.DeviceIdType.MESH)

        copy().start()
        sent[when].append(copy)

    def arrive(dst, sem):
        pltpu.make_async_remote_copy(
            src_ref=dst, dst_ref=dst, send_sem=send_sem.at[0], recv_sem=sem,
            device_id=sibling, device_id_type=pl.DeviceIdType.MESH).wait_recv()

    def load(src, dst, i):
        return pltpu.make_async_copy(src, dst, load_sem.at[i])

    load_w = lambda: load(w_ref, w_v, 0)
    load_q = lambda: load(x_ref.at[0], q_v, 1)
    load_kv = lambda: load(kv_ref, kv_v, 2)
    load_own = lambda: load(x_ref.at[0, :, pl.ds(HALF, YC)], g.at[k_me, y], 3)
    load_own_x = lambda: load(x_ref.at[0, :, pl.ds(HALF + YC, XC)], gx.at[k_me, y], 6)

    @pl.when(first)
    def _():
        load_kv().start()
        load_q().start()

    @pl.when(second)
    def _():
        load_own().start()
        load_own_x().start()

    load_w().start()
    barrier = pltpu.get_barrier_semaphore()
    for dx, d_c, d_s in [(dx, d_c, d_s) for d_s in (0, 1) for dx in (0, 1) for d_c in (0, 1)][1:]:
        pl.semaphore_signal(barrier, inc=1, device_id=at(ox if dx else xh, y, oc if d_c else c, osec if d_s else s),
                            device_id_type=pl.DeviceIdType.MESH)
    for other in (up, across, down):
        pl.semaphore_signal(barrier, inc=1, device_id=other, device_id_type=pl.DeviceIdType.MESH)
    pl.semaphore_wait(barrier, 10)

    def piece(k, y_, p):
        return lambda: g.at[k, y_, pl.ds(p * ROWS, ROWS)]

    def piece_sem(k, y_, p):
        return lambda: g_sem.at[k, y_, p]

    def push(when, k, y_, p, to, src=None):
        send(when, src or piece(k, y_, p), piece(k, y_, p), piece_sem(k, y_, p), to)

    def got(k, y_, p):
        arrive(g.at[k, y_, pl.ds(p * ROWS, ROWS)], g_sem.at[k, y_, p])

    def push_x(when, k, y_, to, src=None):
        send(when, src or (lambda: gx.at[k, y_]), lambda: gx.at[k, y_], lambda: gx_sem.at[k, y_], to)

    def push_low(y_, to, src=None):
        send(1, src or (lambda: sa.at[y_]), lambda: sa.at[y_], lambda: sa_sem.at[y_], to)

    def to_first(y_, src=None):
        for to in (here[0], far[0]):
            push_x(1, k_me, y_, to, src or (lambda: sa.at[y_]))

    def low_arrived(y_, to):
        arrive(sa.at[y_], sa_sem.at[y_])
        if to is not None:
            push_low(y_, to)
        to_first(y_)

    def high_arrived(y_, to):
        arrive(gx.at[k_me, y_], gx_sem.at[k_me, y_])
        if to is not None:
            push_x(1, k_me, y_, to)
        push_x(1, k_me, y_, far[1])
        push_x(1, k_me, y_, sibling)

    def far_arrived(y_):
        arrive(gx.at[k_ox, y_], gx_sem.at[k_ox, y_])
        push_x(1, k_ox, y_, sibling)

    def both_arrived(y_):
        for k in (k_me, k_ox):
            arrive(gx.at[k, y_], gx_sem.at[k, y_])
            push_x(0, k, y_, sibling)

    @pl.when(second)
    def _():
        low = [lambda p=p: x_ref.at[0, pl.ds(p * ROWS, ROWS), pl.ds(0, YC)] for p in range(PIECES)]
        high = [lambda p=p: x_ref.at[0, pl.ds(p * ROWS, ROWS), pl.ds(HALF, YC)] for p in range(PIECES)]
        for p in range(PIECES):
            push(1, k_me, y, p, here[0], low[p])
            push(1, k_me, y, p, far[0], low[p])
            push(1, k_me, y, p, up, high[p])
            push(1, k_me, y, p, down, high[p])
        low_x = lambda: x_ref.at[0, :, pl.ds(YC, XC)]
        high_x = lambda: x_ref.at[0, :, pl.ds(HALF + YC, XC)]
        for to in (up, down):
            push_low(y, to, low_x)
            push_x(1, k_me, y, to, high_x)
        to_first(y, low_x)
        for p in range(PIECES):
            push(1, k_me, y, p, far[1], high[p])
            push(1, k_me, y, p, sibling, high[p])
        push_x(1, k_me, y, far[1], high_x)
        push_x(1, k_me, y, sibling, high_x)

    def relay(k, y_, to):
        for p in range(PIECES):
            got(k, y_, p)
            if to is not None:
                push(None, k, y_, p, to)
            push(None, k, y_, p, sibling)

    def row_step(source, y_):
        for a in (0, 1):
            for b in (0, 1):
                send(0, lambda a=a, b=b: source(a * 2 + b), lambda: cg.at[k_me, y_], lambda: cg_sem.at[k_me, y_], row[a, b, 1])
        send(0, lambda: source(k_sib), lambda: cg.at[k_me, y_], lambda: cg_sem.at[k_me, y_], sibling)

    @pl.when(first)
    def _():
        load_kv().wait()
        load_q().wait()
        causal = (lax.rem(lax.broadcasted_iota(jnp.int32, (GROUP * TOK, TOK), 0), TOK)
                  >= lax.broadcasted_iota(jnp.int32, (GROUP * TOK, TOK), 1))
        for h in (0, 2, 1, 3):
            keys = kv_v[0, :, h * HEAD_DIM:(h + 1) * HEAD_DIM]
            values = kv_v[1, :, h * HEAD_DIM:(h + 1) * HEAD_DIM]
            heads = [h * GROUP + i for i in range(GROUP)]
            queries = jnp.concatenate([q_v[:, i * HEAD_DIM:(i + 1) * HEAD_DIM] for i in heads], axis=0)
            scores = lax.dot_general(queries, keys, NT, preferred_element_type=F32) * SCALE
            scores = jnp.where(causal, scores, -1e30)
            shifted = jnp.exp(scores - jnp.max(scores, axis=-1, keepdims=True))
            weights = shifted * (1.0 / jnp.sum(shifted, axis=-1, keepdims=True))
            probs[h] = weights
            mixed = jnp.dot(weights.astype(BF16), values, preferred_element_type=F32).astype(BF16)
            for i, head in enumerate(heads):
                y_, k_, col = place_of_head(head)
                cs[y_, k_, :, col:col + HEAD_DIM] = mixed[i * TOK:(i + 1) * TOK]
        for y_, to in ((yp, up), (ym, down), (y2, across)):
            send(0, lambda y_=y_: cs.at[y_], lambda: c1.at[:, y], lambda: c1_sem.at[y], to)
        row_step(lambda k_: cs.at[y, k_], y)
        cg[k_me, y] = cs[y, k_me]
        def one():
            for y_ in (yp, ym, y2):
                arrive(c1.at[:, y_], c1_sem.at[y_])
                row_step(lambda k_, y_=y_: c1.at[k_, y_], y_)
                cg[k_me, y_] = c1[k_me, y_]
        def two():
            for p in range(PIECES):
                for k in (k_me, k_ox):
                    got(k, y, p)
                    push(0, k, y, p, up)
                    push(0, k, y, p, down)
                for k in (k_me, k_ox):
                    push(0, k, y, p, sibling)
        for z in ((one, two) if CFIRST else (two, one)): z()

    def grad(y_):
        for k in other_k:
            for p in range(PIECES):
                got(k, y_, p)
            arrive(gx.at[k, y_], gx_sem.at[k, y_])
        block = g[:, y_].reshape(4 * TOK, YC)
        block_x = gx[:, y_].reshape(4 * TOK, XC)
        value = lax.dot_general(block, w_v[:, :YC], NT, preferred_element_type=F32)
        value += lax.dot_general(block_x, w_v[:, YC:], NT, preferred_element_type=F32)
        dp[y_] = value.reshape(4, TOK, FEAT).astype(BF16)

        @pl.when(first)
        def _():
            send(0, lambda: dp.at[y_, pl.ds(ox * 2, 2)], lambda: dr_part.at[y_], lambda: part_sem.at[y_], here[1])
            send(0, lambda: dp.at[y_, k_sib], lambda: dr_sib.at[y_], lambda: sib_sem.at[y_], sibling)

        @pl.when(second)
        def _():
            for b in (0, 1):
                send(1, lambda b=b: dp.at[y_, near_k[b]], lambda: dr_sec.at[y_, c], lambda: sec_sem.at[y_, c], near_row[b])

    def grad_far(y_):
        @pl.when(second)
        def _():
            arrive(dr_part.at[y_], part_sem.at[y_])
            for b in (0, 1):
                dr_sec[y_, b] = (dp[y_, far_k[b]].astype(F32) + dr_part[y_, b].astype(F32)).astype(BF16)
                send(1, lambda b=b: dr_sec.at[y_, b], lambda: ds.at[y_, k_me], lambda: ds_sem.at[y_, c], far_row[b])

    def grad_along_y(y_, to):
        for b in (0, 1):
            arrive(dr_sec.at[y_, b], sec_sem.at[y_, b])
            arrive(ds.at[y_, far_k[b]], ds_sem.at[y_, b])
        arrive(dr_sib.at[y_], sib_sem.at[y_])
        ds[y_, k_me] = (dp[y_, k_me].astype(F32) + dr_sec[y_, c].astype(F32)).astype(BF16)
        ds[y_, k_sib] = (dr_sib[y_].astype(F32) + dr_sec[y_, oc].astype(F32)).astype(BF16)
        if to is None:
            dc[y] = ds[y_]
        else:
            send(0, lambda: ds.at[y_], lambda: dc.at[y], lambda: dc_sem.at[y], to)

    def product(k, start, size):
        block = cg[k].reshape(4 * TOK, FEAT)
        value = jnp.dot(block, w_v[:, start:start + size], preferred_element_type=F32)
        return value.reshape(4, TOK, size).astype(BF16)

    def partial(k, n):
        op[n, k] = product(k, n * PART, PART)

    def block_ready(k, a, other):
        def wait():
            for y_ in (y, yp, ym, y2):
                arrive(cg.at[k, y_], cg_sem.at[k, y_])

        if other:
            pl.when(jnp.logical_or(first, xh == a))(wait)
        else:
            pl.when(jnp.logical_or(jnp.logical_and(first, xh != a), jnp.logical_and(second, xh == a)))(wait)

    def out_x_first():
        for a in (0, 1):
            block_ready(other_k[a], a, True)
            px[other_k[a]] = product(other_k[a], YC, XC)
            send(None, lambda a=a: px.at[other_k[a]], lambda a=a: rx.at[a], lambda a=a: rx_sem.at[a], sibling)
        for a in (0, 1):
            block_ready(own_k[a], a, False)
            px[own_k[a]] = product(own_k[a], YC, XC)

        def total_x(a):
            arrive(rx.at[a], rx_sem.at[a])
            px[own_k[a]] = (px[own_k[a]].astype(F32) + rx[a].astype(F32)).astype(BF16)

        for a in (0, 1):
            total_x(a)

        @pl.when(first)
        def _():
            for a in (0, 1):
                send(0, lambda a=a: px.at[own_k[a]], lambda: xx.at[xh], lambda: xx_sem.at[xh], row_own[a])

        @pl.when(second)
        def _():
            send(1, lambda: px.at[k_ox], lambda: xx.at[2], lambda: xx_sem.at[2], far[1])

    def total(n, a, y_, extra):
        arrive(ra.at[n, a, y_], ra_sem.at[n, a, y_])
        k = own_k[a]
        value = op[n, k, y_].astype(F32) + ra[n, a, y_].astype(F32)
        for ref, i in extra:
            value += ref[n, i].astype(F32)
        op[n, k, y_] = value.astype(BF16)

    def pass_on(n, a, y_, buffer, sems, i, to):
        send(None, lambda: op.at[n, own_k[a], y_], lambda: buffer.at[n, i], lambda: sems.at[n, i], to)

    def out_first(n):
        total(n, 0, y2, [])
        pass_on(n, 0, y2, fwd, f_sem, 0, up)
        total(n, 1, y2, [])
        pass_on(n, 1, y2, bwd, b_sem, 0, down)

    def out_direct(n):
        total(n, 1, yp, [])
        pass_on(n, 1, yp, fwd, f_sem, 1, up)
        total(n, 0, ym, [])
        pass_on(n, 0, ym, bwd, b_sem, 1, down)

    def out_relay(n):
        arrive(fwd.at[n, 0], f_sem.at[n, 0])
        total(n, 0, yp, [(fwd, 0)])
        pass_on(n, 0, yp, fwd, f_sem, 2, up)
        arrive(bwd.at[n, 0], b_sem.at[n, 0])
        total(n, 1, ym, [(bwd, 0)])
        pass_on(n, 1, ym, bwd, b_sem, 2, down)

    def out_along_x(n):
        for i in (1, 2):
            arrive(fwd.at[n, i], f_sem.at[n, i])
            arrive(bwd.at[n, i], b_sem.at[n, i])
        total(n, 0, y, [(fwd, 2), (bwd, 1)])
        total(n, 1, y, [(fwd, 1), (bwd, 2)])

        @pl.when(first)
        def _():
            for a in (0, 1):
                send(0, lambda a=a: op.at[n, own_k[a], y], lambda: xr.at[n, xh], lambda: xr_sem.at[n, xh], row_own[a])

        @pl.when(second)
        def _():
            send(1, lambda: op.at[n, k_ox, y], lambda: xr.at[n, 2], lambda: xr_sem.at[n, 2], far[1])

    load_w().wait()

    @pl.when(second)
    def _():
        load_own().wait()
        load_own_x().wait()

    def out_half(n):
        for a in (0, 1):
            partial(other_k[a], n)
            for y_ in (y2, yp, ym, y):
                send(None, lambda a=a, y_=y_: op.at[n, other_k[a], y_], lambda a=a, y_=y_: ra.at[n, a, y_],
                     lambda a=a, y_=y_: ra_sem.at[n, a, y_], sibling)
        for a in (0, 1):
            partial(own_k[a], n)
        out_first(n)
        out_direct(n)

    def early(name):
        if name == "r1":
            relay(k_me, y_from, toward)
        elif name == "s1":
            @pl.when(second)
            def _():
                low_arrived(ym, up)
                high_arrived(yp, down)
                for p in range(PIECES):
                    got(k_ox, y, p)
                    push(1, k_ox, y, p, up)
                    push(1, k_ox, y, p, down)
                    push(1, k_ox, y, p, sibling)
        elif name == "r2":
            relay(k_ox, y_to, backward)
        elif name == "s2":
            @pl.when(first)
            def _():
                both_arrived(y)

            @pl.when(second)
            def _():
                low_arrived(yp, None)
                high_arrived(ym, None)
                far_arrived(y)
        elif name == "cr":
            @pl.when(second)
            def _():
                for y_ in (y, yp, ym, y2):
                    for k in far_k:
                        arrive(cg.at[k, y_], cg_sem.at[k, y_])
                        send(1, lambda k=k, y_=y_: cg.at[k, y_], lambda k=k, y_=y_: cg.at[k, y_],
                             lambda k=k, y_=y_: cg_sem.at[k, y_], here[0])
        elif name == "gY":
            grad(y)
        elif name == "px":
            out_x_first()
        elif name in ("p0", "p1"):
            out_half(int(name[1]))

    def along_y(i, y_, extra, buffer, sems, slot, to):
        if i == 0:
            value = xx[0, y_].astype(F32) + xx[1, y_].astype(F32)
        else:
            value = xx[2, y_].astype(F32) + px[k_me, y_].astype(F32)
        for ref, at_ in extra:
            value += ref[at_].astype(F32)
        if to is None:
            return value.astype(BF16)
        xx[i, y_] = value.astype(BF16)
        send(1, lambda: xx.at[i, y_], lambda: buffer.at[slot], lambda: sems.at[slot], to)

    def steps(name):
        if name == "rA":
            relay(own_k[1], ym, None)
            relay(own_k[0], yp, None)
        elif name == "xA":
            @pl.when(first)
            def _():
                both_arrived(yp)
                both_arrived(ym)

            @pl.when(second)
            def _():
                low_arrived(y2, None)
                high_arrived(y2, None)
                far_arrived(yp)
                far_arrived(ym)
        elif name == "rB":
            relay(own_k[0], y2, None)
            relay(own_k[1], y2, None)
        elif name == "xB":
            @pl.when(first)
            def _():
                both_arrived(y2)

            @pl.when(second)
            def _():
                far_arrived(y2)
        elif name == "gy":
            grad_far(y)
        elif name == "gA":
            grad(yp)
            grad(ym)
        elif name == "gB":
            grad(y2)
        elif name == "hA":
            grad_far(yp)
            grad_far(ym)
        elif name == "hB":
            grad_far(y2)
        elif name == "lA":
            @pl.when(first)
            def _():
                grad_along_y(yp, up)
                grad_along_y(ym, down)
        elif name == "lB":
            @pl.when(first)
            def _():
                grad_along_y(y2, across)
                grad_along_y(y, None)
        elif name == "T":
            @pl.when(second)
            def _():
                for i in range(3):
                    arrive(xx.at[i], xx_sem.at[i])
                along_y(0, y2, [], xf, xf_sem, 0, up)
                along_y(2, y2, [], xb, xb_sem, 0, down)
                along_y(0, ym, [], xb, xb_sem, 1, down)
                along_y(2, yp, [], xf, xf_sem, 1, up)
        elif name == "X":
            @pl.when(second)
            def _():
                arrive(xf.at[0], xf_sem.at[0])
                along_y(0, yp, [(xf, 0)], xf, xf_sem, 2, up)
                arrive(xb.at[0], xb_sem.at[0])
                along_y(2, ym, [(xb, 0)], xb, xb_sem, 2, down)
        elif name in ("o0", "o1"):
            out_relay(int(name[1]))
        elif name in ("a0", "a1"):
            out_along_x(int(name[1]))
        elif name == "dw":
            ct[...] = cg[...].reshape(16 * TOK, FEAT).T
            weight_grad(g, YC, 0)
            weight_grad(gx, XC, YC)

    def weight_grad(source, size, start):
        @pl.loop(0, size // FEAT)
        def _(n):
            cols = pl.ds(pl.multiple_of(n * FEAT, FEAT), FEAT)
            place = pl.ds(pl.multiple_of(start + n * FEAT, FEAT), FEAT)
            block = source[:, :, :, cols].reshape(16 * TOK, FEAT)
            dw_ref[:, place] = jnp.dot(ct[...], block, preferred_element_type=F32).astype(BF16)

    for name in EARLY + ORDER:
        early(name)
        steps(name)

    @pl.when(first)
    def _():
        for y_ in (yp, ym, y2):
            arrive(dc.at[y_], dc_sem.at[y_])
        for h in range(KV_HEADS):
            keys = kv_v[0, :, h * HEAD_DIM:(h + 1) * HEAD_DIM]
            values = kv_v[1, :, h * HEAD_DIM:(h + 1) * HEAD_DIM]
            heads = [h * GROUP + i for i in range(GROUP)]
            parts = []
            for head in heads:
                y_, k_, col = place_of_head(head)
                parts.append(dc[y_, k_, :, col:col + HEAD_DIM])
            grads = jnp.concatenate(parts, axis=0)
            grad_probs = lax.dot_general(grads, values, NT, preferred_element_type=F32)
            weights = probs[h]
            mean = jnp.sum(weights * grad_probs, axis=-1, keepdims=True)
            grad_scores = (weights * (grad_probs - mean) * SCALE).astype(BF16)
            grad_queries = jnp.dot(grad_scores, keys, preferred_element_type=F32).astype(BF16)
            for i, head in enumerate(heads):
                out_ref[0, :, head * HEAD_DIM:(head + 1) * HEAD_DIM] = grad_queries[i * TOK:(i + 1) * TOK]

    @pl.when(second)
    def _():
        for i in (1, 2):
            arrive(xf.at[i], xf_sem.at[i])
            arrive(xb.at[i], xb_sem.at[i])
        out_ref[0, :, YC:HALF] = along_y(0, y, [(xf, 2), (xb, 1)], None, None, None, None)
        out_ref[0, :, HALF + YC:] = along_y(2, y, [(xf, 1), (xb, 2)], None, None, None, None)
        for n in (0, 1):
            for i in range(3):
                arrive(xr.at[n, i], xr_sem.at[n, i])
            out_ref[0, :, n * PART:(n + 1) * PART] = (xr[n, 0].astype(F32) + xr[n, 1].astype(F32)).astype(BF16)
            out_ref[0, :, HALF + n * PART:HALF + (n + 1) * PART] = (xr[n, 2].astype(F32) + op[n, k_me, y].astype(F32)).astype(BF16)


    for copy in sent[None]:
        copy().wait_send()
    for which in (0, 1):
        @pl.when(s == which)
        def _():
            for copy in sent[which]:
                copy().wait_send()


def body(section_inputs, keys_values, out_weight):
    dma = pltpu.SemaphoreType.DMA
    scratch = [
        pltpu.VMEM((TOK, 4096), BF16),
        pltpu.VMEM((2, TOK, 512), BF16),
        pltpu.VMEM((FEAT, HALF), BF16),
        pltpu.VMEM((KV_HEADS, GROUP * TOK, TOK), F32),
        pltpu.VMEM((4, 4, TOK, FEAT), BF16),
        pltpu.VMEM((4, 4, TOK, FEAT), BF16),
        pltpu.VMEM((4, 4, TOK, FEAT), BF16),
        pltpu.VMEM((FEAT, 16 * TOK), BF16),
        pltpu.VMEM((4, 4, TOK, YC), BF16),
        pltpu.VMEM((4, 4, TOK, XC), BF16),
        pltpu.VMEM((4, TOK, XC), BF16),
        pltpu.VMEM((2, 4, 4, TOK, PART), BF16),
        pltpu.VMEM((2, 2, 4, TOK, PART), BF16),
        pltpu.VMEM((2, 3, TOK, PART), BF16),
        pltpu.VMEM((2, 3, TOK, PART), BF16),
        pltpu.VMEM((2, 3, TOK, PART), BF16),
        pltpu.VMEM((4, 4, TOK, XC), BF16),
        pltpu.VMEM((2, 4, TOK, XC), BF16),
        pltpu.VMEM((3, 4, TOK, XC), BF16),
        pltpu.VMEM((3, TOK, XC), BF16),
        pltpu.VMEM((3, TOK, XC), BF16),
        pltpu.VMEM((4, 4, TOK, FEAT), BF16),
        pltpu.VMEM((4, 2, TOK, FEAT), BF16),
        pltpu.VMEM((4, TOK, FEAT), BF16),
        pltpu.VMEM((4, 2, TOK, FEAT), BF16),
        pltpu.VMEM((4, 4, TOK, FEAT), BF16),
        pltpu.VMEM((4, 4, TOK, FEAT), BF16),
        dma((256,)), dma((7,)), dma((4, 4, PIECES)), dma((4, 4)), dma((4,)), dma((4,)), dma((4, 4)), dma((2, 2, 4)), dma((2, 3)), dma((2, 3)), dma((2, 3)),
        dma((2,)), dma((3,)), dma((3,)), dma((3,)),
        dma((4,)), dma((4,)), dma((4, 2)), dma((4, 2)), dma((4,)),
    ]
    anywhere = pl.BlockSpec(memory_space=pl.ANY)
    return pl.pallas_call(
        kernel,
        out_shape=(pltpu.VMEM(section_inputs.shape, BF16), pltpu.VMEM(out_weight.shape, BF16)),
        in_specs=[anywhere] * 3,
        out_specs=(pl.BlockSpec(memory_space=pltpu.VMEM), pl.BlockSpec(memory_space=pltpu.VMEM)),
        scratch_shapes=scratch,
        compiler_params=pltpu.CompilerParams(
            collective_id=0, has_side_effects=True, vmem_limit_bytes=LIMIT * 1024 * 1024),
        cost_estimate=pl.CostEstimate(flops=3 * 2 * 1024 * 256 * 2048, bytes_accessed=4 << 20, transcendentals=1 << 17),
    )(section_inputs, keys_values, out_weight)


def solution(mesh):
    placed = (
        P("section", ("pair", "shard"), None),
        P(None, ("pair", "shard"), None),
        P("shard", "section"),
    )
    return jax.shard_map(
        body,
        mesh=mesh,
        in_specs=placed,
        out_specs=(P("section", ("pair", "shard"), None), P(("pair", "shard"), "section")),
        check_vma=False,
    )
```
